256 devices in a mesh: loop: 32 (over x, z), group: 8 (over y, core).
Axes of the slice: x: 4, y: 4, z: 8, core: 2. Of those that a mesh axis runs over, the one named last changes fastest.
Arguments:
- features: bfloat16 [6144, 256], P(('loop', 'group')), may hold values from -6 to 6
- scale_exponents: int32 [8], replicated, may hold values from -1 to 2
- targets: int32 [6144], P(('loop', 'group')), may hold values from 0 to 262143
- centres: bfloat16 [262144, 256], P(('loop', 'group')), may hold values from -1 to 1
Outputs:
- row_loss: float32 [6144], P(('loop', 'group'))
- feature_grad: float32 [6144, 256], P(('loop', 'group'))
The draws below stay inside these ranges and needn't reach their ends.
All inputs are finite; a program needn't handle non-finite values.
Results may differ from the reference program's by a relative error of at most 0.015.
Values may be sent and summed in bfloat16 or wider, within the bound.
A program may use at most 192 MiB of HBM per device.

```python
import jax
import jax.numpy as jnp
from jax import lax

D = 256
QB = 32
C = 262144
ROWS = 6144


def sign_patterns(key):
    return jnp.where(jax.random.bernoulli(key, 0.5, (4, D)), 1.0, -1.0).astype(jnp.float32)


def draw_features(key, part):
    patterns = sign_patterns(key)
    key = jax.random.fold_in(key, 21)
    values = jnp.clip(1.5 * jax.random.normal(key, (ROWS, D), jnp.float32), -6.0, 6.0)
    row_index = jnp.arange(ROWS)
    chosen = patterns[row_index // 64 % 4]
    values = jnp.where((row_index % 64 == 0)[:, None], 6.0 * chosen, values)
    return values.astype(jnp.bfloat16)


def draw_centres(key, part):
    patterns = sign_patterns(key)
    key = jax.random.fold_in(key, 22)
    values = jnp.clip(0.25 * jax.random.normal(key, (C, D), jnp.float32), -1.0, 1.0)
    strength = jnp.array([1.0, 0.9, 0.8, 0.7], jnp.float32)[:, None]
    flipped = patterns.at[:, 0].multiply(-1.0)
    class_ids = jnp.arange(4) * (C // 4)
    values = values.at[class_ids].set(strength * patterns)
    values = values.at[class_ids + 1].set(strength * flipped)
    return values.astype(jnp.bfloat16)


def set_ends(entries, own_key, smallest, top_value):
    longest = entries.shape.index(max(entries.shape))
    spots = []
    for shift in (0, 1):
        where = [jax.random.randint(jax.random.fold_in(own_key, axis), (), 0, length) for axis, length in enumerate(entries.shape)]
        where[longest] = (where[longest] + shift) % entries.shape[longest]
        spots.append(tuple(where))
    return entries.at[spots[0]].set(smallest).at[spots[1]].set(top_value)


def setup_inputs(seed: int = 0) -> dict:
    key_of = jax.random.split(jax.random.key(seed), 5)
    return {
        "features": draw_features(jax.random.fold_in(key_of[4], 71), 0),
        "scale_exponents": set_ends(jax.random.randint(key_of[1], (D // QB,), -1, 3), jax.random.fold_in(key_of[1], 1), -1, 2).astype(jnp.int32),
        "targets": set_ends(jax.random.randint(key_of[2], (ROWS,), 0, C), jax.random.fold_in(key_of[2], 1), 0, C - 1).astype(jnp.int32),
        "centres": draw_centres(jax.random.fold_in(key_of[4], 71), 0),
    }


def reference(features, scale_exponents, targets, centres):
    quant_scale = jnp.repeat(jnp.exp2(scale_exponents.astype(jnp.float32)), QB)
    squashed = jnp.tanh(features.astype(jnp.float32) / quant_scale)
    student = (quant_scale * squashed).astype(jnp.bfloat16)
    block_size = min(C, 8192)
    blocks = centres.reshape(C // block_size, block_size, D)

    def class_block(carried, block):
        running_max, exp_total, accum = carried
        logits = lax.dot_general(student, block, (((1,), (1,)), ((), ())), preferred_element_type=jnp.float32)
        new_max = jnp.maximum(running_max, jnp.max(logits, axis=1))
        rescale = jnp.exp(running_max - new_max)
        weights = jnp.exp(logits - new_max[:, None])
        exp_total = exp_total * rescale + jnp.sum(weights, axis=1)
        accum = accum * rescale[:, None] + jnp.dot(weights.astype(jnp.bfloat16), block, preferred_element_type=jnp.float32)
        return (new_max, exp_total, accum), None

    start_state = (jnp.full((ROWS,), -jnp.inf, jnp.float32), jnp.zeros((ROWS,), jnp.float32), jnp.zeros((ROWS, D), jnp.float32))
    (running_max, exp_total, accum), _ = lax.scan(class_block, start_state, blocks)
    picked = jnp.take(centres, targets, axis=0).astype(jnp.float32)
    target_logit = jnp.sum(student.astype(jnp.float32) * picked, axis=1)
    row_loss = running_max + jnp.log(exp_total) - target_logit
    feature_grad = (accum / exp_total[:, None] - picked) * (1.0 - squashed * squashed)
    return row_loss, feature_grad
```

```python
import jax
import jax.numpy as jnp
from jax import lax
from jax.experimental import pallas as pl
from jax.experimental.pallas import tpu as pltpu
from jax.sharding import PartitionSpec as P

F32 = jnp.float32
BF16 = jnp.bfloat16
MESH = pl.DeviceIdType.MESH

NX, NY, NZ = 4, 4, 8
NL = NX * NZ
D = 256
QB = 32
OWN = 24
ROWS = OWN * NL
HALF = 512
UNITS = 16
RT = 256
GR = ROWS // 128


def rcopy(src, dst, send, recv, device):
    return pltpu.make_async_remote_copy(
        src_ref=src, dst_ref=dst, send_sem=send, recv_sem=recv, device_id=device, device_id_type=MESH
    )


def joined(tile):
    return jnp.concatenate([tile[:8], tile[8:]], axis=1)


def parted(rows):
    return jnp.concatenate([rows[:, :128], rows[:, 128:]], axis=0)


def kernel(
    exps, tgts, feats, cents, loss_out, grad_out,
    cbuf, ag_a, ag_b, tgb, s32, sbf, tcol, m, l, acc, t, lcol,
    sx, sz, pk_a, pk_b, rx_a, rz_b, q_a, q_b, rz_a, rx_b,
    c_sem, ring_send, unit_recv,
    a1s, a1r, b1s, b1r, t1s, t1r, a2s, a2r, b2s, b2r, t2s, t2r,
    sxs, sxr, szs, szr, ras, rar, rbs, rbr, rcs, rcr, rds, rdr,
):
    loop = lax.axis_index("loop")
    group = lax.axis_index("group")
    x, z = loop // NZ, loop % NZ
    y, core = group // 2, group % 2
    other = 1 - core
    sibling = (loop, y * 2 + other)
    up = (loop, ((y + 1) % NY) * 2 + core)
    down = (loop, ((y + NY - 1) % NY) * 2 + core)

    def at_x(dx):
        return (((x + dx) % NX) * NZ + z, group)

    def at_z(dz):
        return (x * NZ + (z + dz) % NZ, group)

    barrier = pltpu.get_barrier_semaphore()
    partners = [sibling, up, down] + [at_x(d) for d in range(1, NX)] + [at_z(d) for d in range(1, NZ)]
    for partner in partners:
        pl.semaphore_signal(barrier, inc=1, device_id=partner, device_id_type=MESH)

    own = [
        pltpu.make_async_copy(cents.at[pl.ds(h * HALF, HALF)], cbuf.at[h], c_sem.at[h]) for h in range(2)
    ]
    for copy in own:
        copy.start()

    block = lax.broadcasted_iota(jnp.int32, (1, D), 1) // QB
    scale = jnp.zeros((1, D), F32)
    for b in range(D // QB):
        e = exps[b]
        power = jnp.where(e < 0, 0.5, jnp.where(e < 1, 1.0, jnp.where(e < 2, 2.0, 4.0)))
        scale = jnp.where(block == b, power, scale)
    squashed = jnp.tanh(feats[...].astype(F32) / scale)
    student = (scale * squashed).astype(BF16).astype(F32)
    for k in range(2):
        ag_a[loop, k] = parted(student[8 * k : 8 * k + 8]).astype(BF16)
    ag_b[z * NX + x] = parted(student[16:24]).astype(BF16)
    lane = lax.broadcasted_iota(jnp.int32, (1, 128), 1)
    ids = jnp.zeros((1, 128), jnp.int32)
    for i in range(OWN):
        ids = jnp.where(lane == i, tgts[i], ids)
    tgb[loop] = ids

    pl.semaphore_wait(barrier, len(partners))

    sends = []

    def go(copy):
        copy.start()
        sends.append(copy)

    for d in range(1, NZ):
        go(rcopy(ag_a.at[loop], ag_a.at[loop], a1s.at[d - 1], a1r.at[d - 1], at_z(d)))
        go(rcopy(tgb.at[loop], tgb.at[loop], t1s.at[d - 1], t1r.at[d - 1], at_z(d)))
    for d in range(1, NX):
        slot = z * NX + x
        go(rcopy(ag_b.at[slot], ag_b.at[slot], b1s.at[d - 1], b1r.at[d - 1], at_x(d)))

    for copy in own:
        copy.wait()
    go(rcopy(cbuf.at[0], cbuf.at[4], ring_send.at[0], unit_recv.at[4], up))
    go(rcopy(cbuf.at[1], cbuf.at[5], ring_send.at[1], unit_recv.at[5], down))
    go(rcopy(cbuf.at[0], cbuf.at[2], ring_send.at[2], unit_recv.at[2], sibling))
    go(rcopy(cbuf.at[1], cbuf.at[3], ring_send.at[3], unit_recv.at[3], sibling))
    go(rcopy(cbuf.at[1], cbuf.at[6], ring_send.at[4], unit_recv.at[6], up))
    go(rcopy(cbuf.at[0], cbuf.at[7], ring_send.at[5], unit_recv.at[7], down))

    for d in range(1, NZ):
        slot = x * NZ + (z + NZ - d) % NZ
        rcopy(ag_a.at[slot], ag_a.at[slot], a1s.at[d - 1], a1r.at[d - 1], at_z(d)).wait_recv()
        rcopy(tgb.at[slot], tgb.at[slot], t1s.at[d - 1], t1r.at[d - 1], at_z(d)).wait_recv()
    line = pl.ds(x * NZ, NZ)
    for d in range(1, NX):
        go(rcopy(ag_a.at[line], ag_a.at[line], a2s.at[d - 1], a2r.at[d - 1], at_x(d)))
        go(rcopy(tgb.at[line], tgb.at[line], t2s.at[d - 1], t2r.at[d - 1], at_x(d)))
    for d in range(1, NX):
        slot = z * NX + (x + NX - d) % NX
        rcopy(ag_b.at[slot], ag_b.at[slot], b1s.at[d - 1], b1r.at[d - 1], at_x(d)).wait_recv()
    line = pl.ds(z * NX, NX)
    for d in range(1, NZ):
        go(rcopy(ag_b.at[line], ag_b.at[line], b2s.at[d - 1], b2r.at[d - 1], at_z(d)))

    m[...] = jnp.full_like(m, -1e30)
    l[...] = jnp.zeros_like(l)
    acc[...] = jnp.zeros_like(acc)
    t[...] = jnp.zeros_like(t)

    for d in range(1, NX):
        line = pl.ds(((x + NX - d) % NX) * NZ, NZ)
        rcopy(ag_a.at[line], ag_a.at[line], a2s.at[d - 1], a2r.at[d - 1], at_x(d)).wait_recv()
        rcopy(tgb.at[line], tgb.at[line], t2s.at[d - 1], t2r.at[d - 1], at_x(d)).wait_recv()
    for d in range(1, NZ):
        line = pl.ds(((z + NZ - d) % NZ) * NX, NX)
        rcopy(ag_b.at[line], ag_b.at[line], b2s.at[d - 1], b2r.at[d - 1], at_z(d)).wait_recv()

    eye = lax.broadcasted_iota(jnp.int32, (OWN, 128), 0) == lax.broadcasted_iota(jnp.int32, (OWN, 128), 1)

    def unpack(k, _):
        base = pl.multiple_of(k * OWN, 8)
        s32[pl.ds(base, 8), :] = joined(ag_a[k, 0].astype(F32))
        s32[pl.ds(base + 8, 8), :] = joined(ag_a[k, 1].astype(F32))
        s32[pl.ds(base + 16, 8), :] = joined(ag_b[(k % NZ) * NX + k // NZ].astype(F32))
        row = tgb[k].astype(F32)
        column = jnp.sum(jnp.where(eye, row, 0.0), axis=1, keepdims=True)
        tcol[pl.ds(base, OWN), :] = jnp.broadcast_to(column.astype(jnp.int32), (OWN, 128))
        return 0

    lax.fori_loop(0, NL, unpack, 0)
    sbf[...] = s32[...].astype(BF16)

    lanes = lax.broadcasted_iota(jnp.int32, (1, 128), 1)

    def unit(u, base):
        cb = cbuf[u]

        def row_tile(i, _):
            rows = pl.ds(pl.multiple_of(i * RT, RT), RT)
            logits = lax.dot_general(
                sbf[rows, :], cb, (((1,), (1,)), ((), ())), preferred_element_type=F32
            )
            old = m[rows, :]
            new = jnp.maximum(old, jnp.max(logits, axis=1, keepdims=True))
            fade = jnp.exp(old - new)
            m[rows, :] = new
            total = l[rows, :] * fade
            where = tcol[rows, :] - base
            weights, hits = [], []
            for k in range(HALF // 128):
                w = jnp.exp(logits[:, k * 128 : (k + 1) * 128] - new)
                total = total + w
                weights.append(w.astype(BF16))
                hits.append(jnp.where(where == lanes + k * 128, 1.0, 0.0).astype(BF16))
            l[rows, :] = total
            acc[rows, :] = acc[rows, :] * jnp.concatenate([fade, fade], axis=1) + jnp.dot(
                jnp.concatenate(weights, axis=1), cb, preferred_element_type=F32
            )
            t[rows, :] += jnp.dot(jnp.concatenate(hits, axis=1), cb, preferred_element_type=F32)
            return 0

        lax.fori_loop(0, ROWS // RT, row_tile, 0, unroll=True)

    def base_of(dy, c, h):
        return (loop * 2 * NY + ((y + dy) % NY) * 2 + c) * (2 * HALF) + h * HALF

    def arrive(u):
        rcopy(cbuf.at[u], cbuf.at[u], ring_send.at[0], unit_recv.at[u], sibling).wait_recv()

    def run(first, parts):
        def step(j, _):
            base = jnp.int32(0)
            for n, (dy, c, h) in enumerate(parts):
                base = jnp.where(j == n, base_of(dy, c, h), base)
            unit(first + j, base)
            return 0

        lax.fori_loop(0, len(parts), step, 0)

    run(0, [(0, core, 0), (0, core, 1)])
    arrive(2)
    arrive(3)
    run(2, [(0, other, 0), (0, other, 1)])
    arrive(4)
    go(rcopy(cbuf.at[4], cbuf.at[12], ring_send.at[6], unit_recv.at[12], up))
    go(rcopy(cbuf.at[4], cbuf.at[8], ring_send.at[8], unit_recv.at[8], sibling))
    arrive(5)
    go(rcopy(cbuf.at[5], cbuf.at[13], ring_send.at[7], unit_recv.at[13], down))
    go(rcopy(cbuf.at[5], cbuf.at[9], ring_send.at[9], unit_recv.at[9], sibling))
    run(4, [(3, core, 0), (1, core, 1)])
    arrive(6)
    go(rcopy(cbuf.at[6], cbuf.at[10], ring_send.at[10], unit_recv.at[10], sibling))
    arrive(7)
    go(rcopy(cbuf.at[7], cbuf.at[11], ring_send.at[11], unit_recv.at[11], sibling))
    run(6, [(3, core, 1), (1, core, 0)])
    for u in range(8, 12):
        arrive(u)
    run(8, [(3, other, 0), (1, other, 1), (3, other, 1), (1, other, 0)])
    arrive(12)
    go(rcopy(cbuf.at[12], cbuf.at[14], ring_send.at[12], unit_recv.at[14], sibling))
    arrive(13)
    go(rcopy(cbuf.at[13], cbuf.at[15], ring_send.at[13], unit_recv.at[15], sibling))
    run(12, [(2, core, 0), (2, core, 1)])
    arrive(14)
    arrive(15)
    run(14, [(2, other, 0), (2, other, 1)])

    eye128 = lax.broadcasted_iota(jnp.int32, (128, 128), 0) == lax.broadcasted_iota(jnp.int32, (128, 128), 1)

    def as_row(column):
        return jnp.sum(jnp.where(eye128, column, 0.0), axis=0, keepdims=True)

    sx[0] = jnp.zeros((16, 128), F32)
    for g in range(GR):
        rows = pl.ds(g * 128, 128)
        lse = m[rows, :] + jnp.log(jnp.sum(l[rows, :], axis=1, keepdims=True))
        hit = jnp.sum(s32[rows, :] * t[rows, :], axis=1, keepdims=True)
        sx[0, g : g + 1, :] = as_row(lse)
        sx[0, 8 + g : 9 + g, :] = as_row(hit)

    def combine(ref, count):
        parts = [ref[k] for k in range(count)]
        top = parts[0]
        for part in parts[1:]:
            top = jnp.maximum(top, part)
        total = jnp.zeros_like(top)
        plain = jnp.zeros_like(top)
        for part in parts:
            total = total + jnp.exp(part - top)
            plain = plain + part
        first = lax.broadcasted_iota(jnp.int32, (16, 128), 0) < 8
        return jnp.where(first, top + jnp.log(total), plain)

    for d in range(1, NX):
        go(rcopy(sx.at[0], sx.at[d], sxs.at[d - 1], sxr.at[d - 1], at_x(d)))
    for d in range(1, NX):
        rcopy(sx.at[d], sx.at[d], sxs.at[d - 1], sxr.at[d - 1], at_x(d)).wait_recv()
    sz[0] = combine(sx, NX)
    for d in range(1, NZ):
        go(rcopy(sz.at[0], sz.at[d], szs.at[d - 1], szr.at[d - 1], at_z(d)))
    for d in range(1, NZ):
        rcopy(sz.at[d], sz.at[d], szs.at[d - 1], szr.at[d - 1], at_z(d)).wait_recv()
    stats = combine(sz, NZ)
    for g in range(GR):
        lcol[pl.ds(g * 128, 128), :] = jnp.broadcast_to(
            jnp.sum(jnp.where(eye128, stats[g : g + 1, :], 0.0), axis=1, keepdims=True), (128, 128)
        )

    def pack(k, _):
        base = pl.multiple_of(k * OWN, 8)
        rows = pl.ds(base, OWN)
        share = jnp.exp(m[rows, :] - lcol[rows, :])
        part = acc[rows, :] * jnp.concatenate([share, share], axis=1) - t[rows, :]
        pk_a[k, 0] = parted(part[0:8]).astype(BF16)
        pk_a[k, 1] = parted(part[8:16]).astype(BF16)
        pk_b[(k % NZ) * NX + k // NZ] = parted(part[16:24]).astype(BF16)
        return 0

    lax.fori_loop(0, NL, pack, 0)
    for d in range(1, NX):
        line = pl.ds(((x + d) % NX) * NZ, NZ)
        go(rcopy(pk_a.at[line], rx_a.at[d - 1], ras.at[d - 1], rar.at[d - 1], at_x(d)))
    for d in range(1, NZ):
        line = pl.ds(((z + d) % NZ) * NX, NX)
        go(rcopy(pk_b.at[line], rz_b.at[d - 1], rbs.at[d - 1], rbr.at[d - 1], at_z(d)))
    for d in range(1, NX):
        rcopy(rx_a.at[d - 1], rx_a.at[d - 1], ras.at[d - 1], rar.at[d - 1], at_x(d)).wait_recv()
    total = pk_a[pl.ds(x * NZ, NZ)].astype(F32)
    for d in range(1, NX):
        total = total + rx_a[d - 1].astype(F32)
    q_a[...] = total.astype(BF16)
    for d in range(1, NZ):
        go(rcopy(q_a.at[(z + d) % NZ], rz_a.at[d - 1], rcs.at[d - 1], rcr.at[d - 1], at_z(d)))
    for d in range(1, NZ):
        rcopy(rz_b.at[d - 1], rz_b.at[d - 1], rbs.at[d - 1], rbr.at[d - 1], at_z(d)).wait_recv()
    total = pk_b[pl.ds(z * NX, NX)].astype(F32)
    for d in range(1, NZ):
        total = total + rz_b[d - 1].astype(F32)
    q_b[...] = total.astype(BF16)
    for d in range(1, NX):
        go(rcopy(q_b.at[(x + d) % NX], rx_b.at[d - 1], rds.at[d - 1], rdr.at[d - 1], at_x(d)))

    wanted = loop * OWN + lax.broadcasted_iota(jnp.int32, (OWN, 128), 0)
    place = lax.broadcasted_iota(jnp.int32, (OWN, 128), 1)
    column = jnp.zeros((OWN, 1), F32)
    for g in range(GR):
        row = stats[g : g + 1, :] - stats[8 + g : 9 + g, :]
        column = column + jnp.sum(jnp.where(place + g * 128 == wanted, row, 0.0), axis=1, keepdims=True)
    loss_out[...] = jnp.sum(jnp.where(eye, column, 0.0), axis=0, keepdims=True)

    for d in range(1, NZ):
        rcopy(rz_a.at[d - 1], rz_a.at[d - 1], rcs.at[d - 1], rcr.at[d - 1], at_z(d)).wait_recv()
    part_a = q_a[z].astype(F32)
    for d in range(1, NZ):
        part_a = part_a + rz_a[d - 1].astype(F32)
    for d in range(1, NX):
        rcopy(rx_b.at[d - 1], rx_b.at[d - 1], rds.at[d - 1], rdr.at[d - 1], at_x(d)).wait_recv()
    part_b = q_b[x].astype(F32)
    for d in range(1, NX):
        part_b = part_b + rx_b[d - 1].astype(F32)
    grad = jnp.concatenate([joined(part_a[0]), joined(part_a[1]), joined(part_b)], axis=0)
    squashed = jnp.tanh(feats[...].astype(F32) / scale)
    grad_out[...] = grad * (1.0 - squashed * squashed)

    for copy in sends:
        copy.wait_send()


def body(features, scale_exponents, targets, centres):
    def dma(*shape):
        return pltpu.SemaphoreType.DMA(shape)

    vx, vz = [dma(NX - 1)] * 2, [dma(NZ - 1)] * 2
    loss, grad = pl.pallas_call(
        kernel,
        out_shape=(jax.ShapeDtypeStruct((1, 128), F32), jax.ShapeDtypeStruct((OWN, D), F32)),
        in_specs=[
            pl.BlockSpec(memory_space=pltpu.SMEM),
            pl.BlockSpec(memory_space=pltpu.SMEM),
            pl.BlockSpec(memory_space=pltpu.VMEM),
            pl.BlockSpec(memory_space=pl.ANY),
        ],
        out_specs=(pl.BlockSpec(memory_space=pltpu.VMEM), pl.BlockSpec(memory_space=pltpu.VMEM)),
        scratch_shapes=[
            pltpu.VMEM((UNITS, HALF, D), BF16),
            pltpu.VMEM((NL, 2, 16, 128), BF16),
            pltpu.VMEM((NL, 16, 128), BF16),
            pltpu.VMEM((NL, 1, 128), jnp.int32),
            pltpu.VMEM((ROWS, D), F32),
            pltpu.VMEM((ROWS, D), BF16),
            pltpu.VMEM((ROWS, 128), jnp.int32),
            pltpu.VMEM((ROWS, 128), F32),
            pltpu.VMEM((ROWS, 128), F32),
            pltpu.VMEM((ROWS, D), F32),
            pltpu.VMEM((ROWS, D), F32),
            pltpu.VMEM((ROWS, 128), F32),
            pltpu.VMEM((NX, 16, 128), F32),
            pltpu.VMEM((NZ, 16, 128), F32),
            pltpu.VMEM((NL, 2, 16, 128), BF16),
            pltpu.VMEM((NL, 16, 128), BF16),
            pltpu.VMEM((NX - 1, NZ, 2, 16, 128), BF16),
            pltpu.VMEM((NZ - 1, NX, 16, 128), BF16),
            pltpu.VMEM((NZ, 2, 16, 128), BF16),
            pltpu.VMEM((NX, 16, 128), BF16),
            pltpu.VMEM((NZ - 1, 2, 16, 128), BF16),
            pltpu.VMEM((NX - 1, 16, 128), BF16),
            dma(2),
            dma(14),
            dma(UNITS),
            *vz, *vx, *vz, *vx, *vz, *vx,
            *vx, *vz, *vx, *vz, *vz, *vx,
        ],
        compiler_params=pltpu.CompilerParams(
            collective_id=0, has_side_effects=True, vmem_limit_bytes=40 * 1024 * 1024
        ),
    )(scale_exponents, targets, features, centres)
    return loss[0, :OWN], grad


def solution(mesh):
    placed = (P(("loop", "group"), None), P(), P(("loop", "group")), P(("loop", "group"), None))
    return jax.shard_map(
        body,
        mesh=mesh,
        in_specs=placed,
        out_specs=(P(("loop", "group")), P(("loop", "group"), None)),
        check_vma=False,
    )
```

```python
import jax
import jax.numpy as jnp
from jax import lax
from jax.experimental import pallas as pl
from jax.experimental.pallas import tpu as pltpu
from jax.sharding import PartitionSpec as P

F32 = jnp.float32
BF16 = jnp.bfloat16
MESH = pl.DeviceIdType.MESH

NX, NY, NZ = 4, 4, 8
NL = NX * NZ
D = 256
QB = 32
OWN = 24
ROWS = OWN * NL
HALF = 512
UNITS = 16
RT = 768
RA = 16 * NL


def rcopy(src, dst, send, recv, device):
    return pltpu.make_async_remote_copy(
        src_ref=src, dst_ref=dst, send_sem=send, recv_sem=recv, device_id=device, device_id_type=MESH
    )


def joined(tiles):
    count = tiles.shape[0]
    low = tiles[:, :8].reshape(count * 8, 128)
    high = tiles[:, 8:].reshape(count * 8, 128)
    return jnp.concatenate([low, high], axis=1)


def parted(rows):
    count = rows.shape[0] // 8
    low = rows[:, :128].reshape(count, 8, 128)
    high = rows[:, 128:].reshape(count, 8, 128)
    return jnp.concatenate([low, high], axis=1)


def shares(parts):
    top = parts[0]
    for part in parts[1:]:
        top = jnp.maximum(top, part)
    powers = [jnp.exp(part - top) for part in parts]
    total = powers[0]
    for power in powers[1:]:
        total = total + power
    return top + jnp.log(total), [power / total for power in powers]


def twice(column):
    wide = jnp.broadcast_to(column, (8, 128))
    return jnp.concatenate([wide, wide], axis=0)


def kernel(
    exps_hbm, tgts_hbm, feats_hbm, cents, loss_out, grad_out,
    exps, tgts, feats, cbuf, ag_a, ag_b, tgb, sbf, tcol, m, l, acc, t,
    pk_a, pk_b, ht_a, ht_b, rht_a, rht_b, la, lb, rx_a, rz_b, rla, rlb, q_a, q_b, qla, qlb, rz_a, rx_b, flA, flB,
    in_sem, c_sem, ring_send, unit_recv,
    a1s, a1r, b1s, b1r, t1s, t1r, a2s, a2r, b2s, b2r, t2s, t2r,
    ras, rar, rbs, rbr, rcs, rcr, rds, rdr,
    has, har, hbs, hbr, las, lar, lbs, lbr, lcs, lcr, lds, ldr,
):
    loop = lax.axis_index("loop")
    group = lax.axis_index("group")
    x, z = loop // NZ, loop % NZ
    y, core = group // 2, group % 2
    other = 1 - core
    sibling = (loop, y * 2 + other)
    up = (loop, ((y + 1) % NY) * 2 + core)
    down = (loop, ((y + NY - 1) % NY) * 2 + core)

    def at_x(dx):
        return (((x + dx) % NX) * NZ + z, group)

    def at_z(dz):
        return (x * NZ + (z + dz) % NZ, group)

    barrier = pltpu.get_barrier_semaphore()
    partners = [at_z(d) for d in range(1, NZ)] + [at_x(d) for d in range(1, NX)] + [sibling, up, down]
    for partner in partners:
        pl.semaphore_signal(barrier, inc=1, device_id=partner, device_id_type=MESH)

    small = [
        pltpu.make_async_copy(exps_hbm, exps, in_sem.at[0]),
        pltpu.make_async_copy(tgts_hbm, tgts, in_sem.at[1]),
        pltpu.make_async_copy(feats_hbm, feats, in_sem.at[2]),
    ]
    own = [
        pltpu.make_async_copy(cents.at[pl.ds(h * HALF, HALF)], cbuf.at[h], c_sem.at[h]) for h in range(2)
    ]
    for copy in small + own:
        copy.start()
    for copy in small:
        copy.wait()

    block = lax.broadcasted_iota(jnp.int32, (1, D), 1) // QB
    scale = jnp.zeros((1, D), F32)
    for b in range(D // QB):
        e = exps[b]
        power = jnp.where(e < 0, 0.5, jnp.where(e < 1, 1.0, jnp.where(e < 2, 2.0, 4.0)))
        scale = jnp.where(block == b, power, scale)
    squashed = jnp.tanh(feats[...].astype(F32) / scale)
    student = (scale * squashed).astype(BF16).astype(F32)
    tiles = parted(student).astype(BF16)
    ag_a[loop] = tiles[0:2]
    ag_b[z * NX + x] = tiles[2]
    lane = lax.broadcasted_iota(jnp.int32, (1, 128), 1)
    ids = jnp.zeros((1, 128), jnp.int32)
    for i in range(OWN):
        ids = jnp.where(lane == i, tgts[i], ids)
    tgb[loop] = ids

    pl.semaphore_wait(barrier, len(partners))

    sends = []

    def go(copy):
        copy.start()
        sends.append(copy)

    for d in range(1, NZ):
        go(rcopy(ag_a.at[loop], ag_a.at[loop], a1s.at[d - 1], a1r.at[d - 1], at_z(d)))
    for d in range(1, NX):
        slot = z * NX + x
        go(rcopy(ag_b.at[slot], ag_b.at[slot], b1s.at[d - 1], b1r.at[d - 1], at_x(d)))

    for copy in own:
        copy.wait()
    go(rcopy(cbuf.at[0], cbuf.at[4], ring_send.at[0], unit_recv.at[4], up))
    go(rcopy(cbuf.at[1], cbuf.at[5], ring_send.at[1], unit_recv.at[5], down))
    go(rcopy(cbuf.at[0], cbuf.at[2], ring_send.at[2], unit_recv.at[2], sibling))
    go(rcopy(cbuf.at[1], cbuf.at[3], ring_send.at[3], unit_recv.at[3], sibling))
    go(rcopy(cbuf.at[1], cbuf.at[6], ring_send.at[4], unit_recv.at[6], up))
    go(rcopy(cbuf.at[0], cbuf.at[7], ring_send.at[5], unit_recv.at[7], down))
    for d in range(1, NZ):
        go(rcopy(tgb.at[loop], tgb.at[loop], t1s.at[d - 1], t1r.at[d - 1], at_z(d)))

    for d in range(1, NZ):
        slot = x * NZ + (z + NZ - d) % NZ
        rcopy(ag_a.at[slot], ag_a.at[slot], a1s.at[d - 1], a1r.at[d - 1], at_z(d)).wait_recv()
    line = pl.ds(x * NZ, NZ)
    for d in range(1, NX):
        go(rcopy(ag_a.at[line], ag_a.at[line], a2s.at[d - 1], a2r.at[d - 1], at_x(d)))
    for d in range(1, NX):
        slot = z * NX + (x + NX - d) % NX
        rcopy(ag_b.at[slot], ag_b.at[slot], b1s.at[d - 1], b1r.at[d - 1], at_x(d)).wait_recv()
    line = pl.ds(z * NX, NX)
    for d in range(1, NZ):
        go(rcopy(ag_b.at[line], ag_b.at[line], b2s.at[d - 1], b2r.at[d - 1], at_z(d)))
    for d in range(1, NZ):
        slot = x * NZ + (z + NZ - d) % NZ
        rcopy(tgb.at[slot], tgb.at[slot], t1s.at[d - 1], t1r.at[d - 1], at_z(d)).wait_recv()
    line = pl.ds(x * NZ, NZ)
    for d in range(1, NX):
        go(rcopy(tgb.at[line], tgb.at[line], t2s.at[d - 1], t2r.at[d - 1], at_x(d)))

    m[...] = jnp.full_like(m, -1e30)
    l[...] = jnp.zeros_like(l)
    acc[...] = jnp.zeros_like(acc)
    t[...] = jnp.zeros_like(t)

    for d in range(1, NX):
        line = pl.ds(((x + NX - d) % NX) * NZ, NZ)
        rcopy(ag_a.at[line], ag_a.at[line], a2s.at[d - 1], a2r.at[d - 1], at_x(d)).wait_recv()
    sbf[0:RA, :] = joined(ag_a[...].astype(F32).reshape(2 * NL, 16, 128)).astype(BF16)
    for d in range(1, NX):
        line = pl.ds(((x + NX - d) % NX) * NZ, NZ)
        rcopy(tgb.at[line], tgb.at[line], t2s.at[d - 1], t2r.at[d - 1], at_x(d)).wait_recv()
    eye = lax.broadcasted_iota(jnp.int32, (OWN, 128), 0) == lax.broadcasted_iota(jnp.int32, (OWN, 128), 1)
    for k in range(NL):
        row = tgb[k].astype(F32)
        column = jnp.sum(jnp.where(eye, row, 0.0), axis=1, keepdims=True).astype(jnp.int32)
        slot = (k % NZ) * NX + k // NZ
        tcol[16 * k : 16 * k + 16, :] = jnp.broadcast_to(column[:16], (16, 128))
        tcol[RA + 8 * slot : RA + 8 * slot + 8, :] = jnp.broadcast_to(column[16:], (8, 128))
    for d in range(1, NZ):
        line = pl.ds(((z + NZ - d) % NZ) * NX, NX)
        rcopy(ag_b.at[line], ag_b.at[line], b2s.at[d - 1], b2r.at[d - 1], at_z(d)).wait_recv()
    sbf[RA:ROWS, :] = joined(ag_b[...].astype(F32)).astype(BF16)

    lanes = lax.broadcasted_iota(jnp.int32, (1, 128), 1)

    def chunk(u, bases, soft=True, pick=True):
        def row_tile(i, _):
            rows = pl.ds(pl.multiple_of(i * RT, RT), RT)
            cb = jnp.concatenate([cbuf[u + n] for n in range(len(bases))], axis=0)
            if soft:
                logits = lax.dot_general(
                    sbf[rows, :], cb, (((1,), (1,)), ((), ())), preferred_element_type=F32
                )
                old = m[rows, :]
                new = jnp.maximum(old, jnp.max(logits, axis=1, keepdims=True))
                fade = jnp.exp(old - new)
                m[rows, :] = new
                total = l[rows, :] * fade
                weights = []
                for k in range(len(bases) * HALF // 128):
                    w = jnp.exp(logits[:, k * 128 : (k + 1) * 128] - new)
                    total = total + w
                    weights.append(w.astype(BF16))
                l[rows, :] = total
                acc[rows, :] = acc[rows, :] * jnp.concatenate([fade, fade], axis=1) + jnp.dot(
                    jnp.concatenate(weights, axis=1), cb, preferred_element_type=F32
                )
            if pick:
                hits = []
                for base in bases:
                    where = tcol[rows, :] - base
                    for k in range(HALF // 128):
                        hits.append(jnp.where(where == lanes + k * 128, 1.0, 0.0).astype(BF16))
                t[rows, :] += jnp.dot(jnp.concatenate(hits, axis=1), cb, preferred_element_type=F32)
            return 0

        lax.fori_loop(0, ROWS // RT, row_tile, 0, unroll=True)

    def bases_of(*parts):
        return [
            (loop * 2 * NY + ((y + dy) % NY) * 2 + c) * (2 * HALF) + h * HALF for dy, c, h in parts
        ]

    def arrive(*units):
        for u in units:
            rcopy(cbuf.at[u], cbuf.at[u], ring_send.at[0], unit_recv.at[u], sibling).wait_recv()

    arrive(4)
    go(rcopy(cbuf.at[4], cbuf.at[12], ring_send.at[6], unit_recv.at[12], up))
    go(rcopy(cbuf.at[4], cbuf.at[8], ring_send.at[8], unit_recv.at[8], sibling))
    arrive(5)
    go(rcopy(cbuf.at[5], cbuf.at[13], ring_send.at[7], unit_recv.at[13], down))
    go(rcopy(cbuf.at[5], cbuf.at[9], ring_send.at[9], unit_recv.at[9], sibling))
    arrive(2, 3)
    chunk(0, bases_of((0, core, 0), (0, core, 1), (0, other, 0), (0, other, 1)))
    arrive(6)
    go(rcopy(cbuf.at[6], cbuf.at[10], ring_send.at[10], unit_recv.at[10], sibling))
    arrive(7)
    go(rcopy(cbuf.at[7], cbuf.at[11], ring_send.at[11], unit_recv.at[11], sibling))
    chunk(4, bases_of((3, core, 0), (1, core, 1), (3, core, 1), (1, core, 0)))
    arrive(8, 9, 10, 11)
    chunk(8, bases_of((3, other, 0), (1, other, 1), (3, other, 1), (1, other, 0)))
    last = bases_of((2, core, 0), (2, core, 1), (2, other, 0), (2, other, 1))
    arrive(12)
    go(rcopy(cbuf.at[12], cbuf.at[14], ring_send.at[12], unit_recv.at[14], sibling))
    arrive(13)
    go(rcopy(cbuf.at[13], cbuf.at[15], ring_send.at[13], unit_recv.at[15], sibling))
    chunk(12, last[:2], pick=False)
    arrive(14, 15)
    chunk(12, last, soft=False)
    for k in range(0, ROWS // 8, 2 * NZ):
        hit = parted(t[8 * k : 8 * k + 16 * NZ, :]).astype(BF16)
        if k < RA // 8:
            ht_a[k // 2 : k // 2 + NZ] = hit.reshape(NZ, 2, 16, 128)
        else:
            ht_b[k - RA // 8 : k - RA // 8 + 2 * NZ] = hit
    for d in range(1, NX):
        to = (x + d) % NX
        go(rcopy(ht_a.at[pl.ds(to * NZ, NZ)], rht_a.at[d - 1], has.at[d - 1], har.at[d - 1], at_x(d)))
    for d in range(1, NZ):
        to = (z + d) % NZ
        go(rcopy(ht_b.at[pl.ds(to * NX, NX)], rht_b.at[d - 1], hbs.at[d - 1], hbr.at[d - 1], at_z(d)))
    chunk(14, last[2:], pick=False)

    block8 = lax.broadcasted_iota(jnp.int32, (8, 128), 1) // 8

    def closed(rows):
        total = jnp.sum(l[rows, :], axis=1, keepdims=True)
        l[rows, :] = m[rows, :] + jnp.log(total)
        return parted(acc[rows, :] * (1.0 / total)).astype(BF16)

    def lanes_of(first, count):
        out = jnp.zeros((8, 128), F32)
        for j in range(count):
            out = jnp.where(block8 == j, l[first + 8 * j : first + 8 * j + 8, :], out)
        return out

    for k in range(NX):
        pk_a[k * NZ : (k + 1) * NZ] = closed(pl.ds(k * 128, 128)).reshape(NZ, 2, 16, 128)
        la[k] = lanes_of(k * 128, 2 * NZ)
    for d in range(1, NX):
        to = (x + d) % NX
        go(rcopy(pk_a.at[pl.ds(to * NZ, NZ)], rx_a.at[d - 1], ras.at[d - 1], rar.at[d - 1], at_x(d)))
        go(rcopy(la.at[to], rla.at[d - 1], las.at[d - 1], lar.at[d - 1], at_x(d)))
    for k in range(0, NZ, 4):
        pk_b[k * NX : (k + 4) * NX] = closed(pl.ds(RA + k * 32, 128))
    for k in range(NZ):
        lb[k] = lanes_of(RA + k * 32, NX)
    for d in range(1, NZ):
        to = (z + d) % NZ
        go(rcopy(pk_b.at[pl.ds(to * NX, NX)], rz_b.at[d - 1], rbs.at[d - 1], rbr.at[d - 1], at_z(d)))
        go(rcopy(lb.at[to], rlb.at[d - 1], lbs.at[d - 1], lbr.at[d - 1], at_z(d)))
    for copy in sends:
        copy.wait_send()
    sends.clear()

    for d in range(1, NX):
        rcopy(rla.at[d - 1], rla.at[d - 1], las.at[d - 1], lar.at[d - 1], at_x(d)).wait_recv()
    for d in range(1, NX):
        rcopy(rht_a.at[d - 1], rht_a.at[d - 1], has.at[d - 1], har.at[d - 1], at_x(d)).wait_recv()
    hit = ht_a[pl.ds(x * NZ, NZ)]
    for d in range(1, NX):
        hit = hit + rht_a[d - 1]
    q_a[:, 1] = hit
    lse, parts = shares([la[x]] + [rla[d - 1] for d in range(1, NX)])
    qla[...] = lse
    for d in range(1, NX):
        rcopy(rx_a.at[d - 1], rx_a.at[d - 1], ras.at[d - 1], rar.at[d - 1], at_x(d)).wait_recv()
    for k in range(NZ):
        got = [pk_a[x * NZ + k]] + [rx_a[d - 1, k] for d in range(1, NX)]
        for j in range(2):
            at = 8 * (2 * k + j)
            mean = jnp.zeros((16, 128), F32)
            for part, tile in zip(parts, got):
                mean = mean + twice(part[:, at : at + 1]) * tile[j].astype(F32)
            q_a[k, 0, j] = mean.astype(BF16)
    for d in range(1, NZ):
        go(rcopy(q_a.at[(z + d) % NZ], rz_a.at[d - 1], rcs.at[d - 1], rcr.at[d - 1], at_z(d)))
        go(rcopy(qla, flA.at[d - 1], lcs.at[d - 1], lcr.at[d - 1], at_z(d)))

    for d in range(1, NZ):
        rcopy(rlb.at[d - 1], rlb.at[d - 1], lbs.at[d - 1], lbr.at[d - 1], at_z(d)).wait_recv()
    for d in range(1, NZ):
        rcopy(rht_b.at[d - 1], rht_b.at[d - 1], hbs.at[d - 1], hbr.at[d - 1], at_z(d)).wait_recv()
    hit = ht_b[pl.ds(z * NX, NX)]
    for d in range(1, NZ):
        hit = hit + rht_b[d - 1]
    q_b[:, 1] = hit
    lse, parts = shares([lb[z]] + [rlb[d - 1] for d in range(1, NZ)])
    qlb[...] = lse
    for d in range(1, NZ):
        rcopy(rz_b.at[d - 1], rz_b.at[d - 1], rbs.at[d - 1], rbr.at[d - 1], at_z(d)).wait_recv()
    for k in range(NX):
        got = [pk_b[z * NX + k]] + [rz_b[d - 1, k] for d in range(1, NZ)]
        mean = jnp.zeros((16, 128), F32)
        for part, tile in zip(parts, got):
            mean = mean + twice(part[:, 8 * k : 8 * k + 1]) * tile.astype(F32)
        q_b[k, 0] = mean.astype(BF16)
    for d in range(1, NX):
        go(rcopy(q_b.at[(x + d) % NX], rx_b.at[d - 1], rds.at[d - 1], rdr.at[d - 1], at_x(d)))
        go(rcopy(qlb, flB.at[d - 1], lds.at[d - 1], ldr.at[d - 1], at_x(d)))

    lane8 = lax.broadcasted_iota(jnp.int32, (8, 128), 1)

    def picked_lane(value, at):
        return jnp.sum(jnp.where(lane8 == at, value, 0.0), axis=1, keepdims=True)

    def finish(lse_parts, own_tile, got, places):
        lse, parts = shares(lse_parts)
        means, hits, lses = [], [], []
        for j, at in enumerate(places):
            mean = jnp.zeros((16, 128), F32)
            hit = jnp.zeros((16, 128), F32)
            for part, tile in zip(parts, [own_tile] + got):
                mean = mean + twice(picked_lane(part, at)) * tile(0, j).astype(F32)
                hit = hit + tile(1, j).astype(F32)
            means.append(mean)
            hits.append(hit)
            lses.append(picked_lane(lse, at))
        return means, hits, lses

    for d in range(1, NX):
        rcopy(flB.at[d - 1], flB.at[d - 1], lds.at[d - 1], ldr.at[d - 1], at_x(d)).wait_recv()
        rcopy(rx_b.at[d - 1], rx_b.at[d - 1], rds.at[d - 1], rdr.at[d - 1], at_x(d)).wait_recv()
    late = finish(
        [qlb[...]] + [flB[d - 1] for d in range(1, NX)],
        lambda n, j: q_b[x, n],
        [lambda n, j, d=d: rx_b[d - 1, n] for d in range(1, NX)],
        [8 * x],
    )
    for d in range(1, NZ):
        rcopy(flA.at[d - 1], flA.at[d - 1], lcs.at[d - 1], lcr.at[d - 1], at_z(d)).wait_recv()
        rcopy(rz_a.at[d - 1], rz_a.at[d - 1], rcs.at[d - 1], rcr.at[d - 1], at_z(d)).wait_recv()
    early = finish(
        [qla[...]] + [flA[d - 1] for d in range(1, NZ)],
        lambda n, j: q_a[z, n, j],
        [lambda n, j, d=d: rz_a[d - 1, n, j] for d in range(1, NZ)],
        [16 * z, 16 * z + 8],
    )
    means, hits, lses = [a + b for a, b in zip(early, late)]
    mean = jnp.concatenate([jnp.concatenate([v[:8], v[8:]], axis=1) for v in means], axis=0)
    hit = jnp.concatenate([jnp.concatenate([v[:8], v[8:]], axis=1) for v in hits], axis=0)
    squashed = jnp.tanh(feats[...].astype(F32) / scale)
    student = (scale * squashed).astype(BF16).astype(F32)
    grad_out[...] = (mean - hit) * (1.0 - squashed * squashed)
    column = jnp.concatenate(lses, axis=0) - jnp.sum(student * hit, axis=1, keepdims=True)
    loss_out[...] = jnp.sum(jnp.where(eye, column, 0.0), axis=0, keepdims=True)

    for copy in sends:
        copy.wait_send()


def body(features, scale_exponents, targets, centres):
    def dma(*shape):
        return pltpu.SemaphoreType.DMA(shape)

    vx, vz = [dma(NX - 1)] * 2, [dma(NZ - 1)] * 2
    loss, grad = pl.pallas_call(
        kernel,
        out_shape=(jax.ShapeDtypeStruct((1, 128), F32), jax.ShapeDtypeStruct((OWN, D), F32)),
        in_specs=[pl.BlockSpec(memory_space=pl.ANY)] * 4,
        out_specs=(pl.BlockSpec(memory_space=pltpu.VMEM), pl.BlockSpec(memory_space=pltpu.VMEM)),
        scratch_shapes=[
            pltpu.SMEM((D // QB,), jnp.int32),
            pltpu.SMEM((OWN,), jnp.int32),
            pltpu.VMEM((OWN, D), BF16),
            pltpu.VMEM((UNITS, HALF, D), BF16),
            pltpu.VMEM((NL, 2, 16, 128), BF16),
            pltpu.VMEM((NL, 16, 128), BF16),
            pltpu.VMEM((NL, 1, 128), jnp.int32),
            pltpu.VMEM((ROWS, D), BF16),
            pltpu.VMEM((ROWS, 128), jnp.int32),
            pltpu.VMEM((ROWS, 128), F32),
            pltpu.VMEM((ROWS, 128), F32),
            pltpu.VMEM((ROWS, D), F32),
            pltpu.VMEM((ROWS, D), F32),
            pltpu.VMEM((NL, 2, 16, 128), BF16),
            pltpu.VMEM((NL, 16, 128), BF16),
            pltpu.VMEM((NL, 2, 16, 128), BF16),
            pltpu.VMEM((NL, 16, 128), BF16),
            pltpu.VMEM((NX - 1, NZ, 2, 16, 128), BF16),
            pltpu.VMEM((NZ - 1, NX, 16, 128), BF16),
            pltpu.VMEM((NX, 8, 128), F32),
            pltpu.VMEM((NZ, 8, 128), F32),
            pltpu.VMEM((NX - 1, NZ, 2, 16, 128), BF16),
            pltpu.VMEM((NZ - 1, NX, 16, 128), BF16),
            pltpu.VMEM((NX - 1, 8, 128), F32),
            pltpu.VMEM((NZ - 1, 8, 128), F32),
            pltpu.VMEM((NZ, 2, 2, 16, 128), BF16),
            pltpu.VMEM((NX, 2, 16, 128), BF16),
            pltpu.VMEM((8, 128), F32),
            pltpu.VMEM((8, 128), F32),
            pltpu.VMEM((NZ - 1, 2, 2, 16, 128), BF16),
            pltpu.VMEM((NX - 1, 2, 16, 128), BF16),
            pltpu.VMEM((NZ - 1, 8, 128), F32),
            pltpu.VMEM((NX - 1, 8, 128), F32),
            dma(3),
            dma(2),
            dma(14),
            dma(UNITS),
            *vz, *vx, *vz, *vx, *vz, *vx,
            *vx, *vz, *vz, *vx,
            *vx, *vz, *vx, *vz, *vz, *vx,
        ],
        compiler_params=pltpu.CompilerParams(
            collective_id=0, has_side_effects=True, vmem_limit_bytes=60 * 1024 * 1024
        ),
    )(scale_exponents, targets, features, centres)
    return loss[0, :OWN], grad


def solution(mesh):
    placed = (P(("loop", "group"), None), P(), P(("loop", "group")), P(("loop", "group"), None))
    return jax.shard_map(
        body,
        mesh=mesh,
        in_specs=placed,
        out_specs=(P(("loop", "group")), P(("loop", "group"), None)),
        check_vma=False,
    )
```

```python
import jax
import jax.numpy as jnp
from jax import lax
from jax.experimental import pallas as pl
from jax.experimental.pallas import tpu as pltpu
from jax.sharding import PartitionSpec as P

F32 = jnp.float32
BF16 = jnp.bfloat16
MESH = pl.DeviceIdType.MESH

NX, NY, NZ = 4, 4, 8
NL = NX * NZ
D = 256
QB = 32
OWN = 24
ROWS = OWN * NL
HALF = 512
UNITS = 16
PART = 8 * NL
FIRST, SECOND = (NZ, NX, NZ), (NX, NZ, NX)
TILE = (0, 2, 1)


def rcopy(src, dst, send, recv, device):
    return pltpu.make_async_remote_copy(
        src_ref=src, dst_ref=dst, send_sem=send, recv_sem=recv, device_id=device, device_id_type=MESH
    )


def joined(tiles):
    count = tiles.shape[0]
    low = tiles[:, :8].reshape(count * 8, 128)
    high = tiles[:, 8:].reshape(count * 8, 128)
    return jnp.concatenate([low, high], axis=1)


def parted(rows):
    count = rows.shape[0] // 8
    low = rows[:, :128].reshape(count, 8, 128)
    high = rows[:, 128:].reshape(count, 8, 128)
    return jnp.concatenate([low, high], axis=1)


def shares(parts):
    top = parts[0]
    for part in parts[1:]:
        top = jnp.maximum(top, part)
    powers = [jnp.exp(part - top) for part in parts]
    total = powers[0]
    for power in powers[1:]:
        total = total + power
    return top + jnp.log(total), [power / total for power in powers]


def twice(column):
    wide = jnp.broadcast_to(column, (8, 128))
    return jnp.concatenate([wide, wide], axis=0)


def kernel(
    exps_hbm, tgts_hbm, feats_hbm, cents, loss_out, grad_out,
    exps, tgts, feats, cbuf, tgb, sbf, tcol, m, l, acc, t, *rest
):
    rest = list(rest)

    def take(count):
        out, rest[:count] = rest[:count], []
        return out

    ag, pk, ht, ls, rx, rht, rls, q, qls, rz, fls, psend, precv, hsend, hrecv = [take(3) for _ in range(15)]
    in_sem, c_sem, ring_send, unit_recv, tsend, trecv = rest
    loop = lax.axis_index("loop")
    group = lax.axis_index("group")
    x, z = loop // NZ, loop % NZ
    y, core = group // 2, group % 2
    other = 1 - core

    def chip(dx, dy, c):
        return (((x + dx + NX) % NX) * NZ + z, ((y + dy + NY) % NY) * 2 + c)

    def along_x(d):
        return chip(d, 0, core)

    def along_z(d):
        return (x * NZ + (z + d) % NZ, group)

    sibling = chip(0, 0, other)
    up, down = chip(0, 1, core), chip(0, -1, core)
    barrier = pltpu.get_barrier_semaphore()
    partners = [along_z(d) for d in range(1, NZ)] + [along_x(d) for d in range(1, NX)]
    partners += [sibling, up, down]
    for partner in partners:
        pl.semaphore_signal(barrier, inc=1, device_id=partner, device_id_type=MESH)

    small = [
        pltpu.make_async_copy(exps_hbm, exps, in_sem.at[0]),
        pltpu.make_async_copy(tgts_hbm, tgts, in_sem.at[1]),
        pltpu.make_async_copy(feats_hbm, feats, in_sem.at[2]),
    ]
    own = [
        pltpu.make_async_copy(cents.at[pl.ds(h * HALF, HALF)], cbuf.at[h], c_sem.at[h]) for h in range(2)
    ]
    for copy in small + own:
        copy.start()
    for copy in small:
        copy.wait()

    hop1 = (along_z, along_x, along_z)
    hop2 = (along_x, along_z, along_x)
    here1, here2 = (z, x, z), (x, z, x)

    block = lax.broadcasted_iota(jnp.int32, (1, D), 1) // QB
    scale = jnp.zeros((1, D), F32)
    for b in range(D // QB):
        e = exps[b]
        power = jnp.where(e < 0, 0.5, jnp.where(e < 1, 1.0, jnp.where(e < 2, 2.0, 4.0)))
        scale = jnp.where(block == b, power, scale)
    squashed = jnp.tanh(feats[...].astype(F32) / scale)
    student = (scale * squashed).astype(BF16).astype(F32)
    tiles = parted(student).astype(BF16)
    for p in range(3):
        ag[p][here2[p] * FIRST[p] + here1[p]] = tiles[TILE[p]]
    lane = lax.broadcasted_iota(jnp.int32, (1, 128), 1)
    ids = jnp.zeros((1, 128), jnp.int32)
    for i in range(OWN):
        ids = jnp.where(lane == i, tgts[i], ids)
    tgb[loop] = ids

    pl.semaphore_wait(barrier, len(partners))

    sends = []

    def go(copy):
        copy.start()
        sends.append(copy)

    def ag1(p, d, slot):
        ref = ag[p].at[slot]
        return rcopy(ref, ref, psend[p].at[d - 1], precv[p].at[d - 1], hop1[p](d))

    def ag2(p, d, place):
        ref = ag[p].at[pl.ds(place * FIRST[p], FIRST[p])]
        sem = FIRST[p] - 2 + d
        return rcopy(ref, ref, psend[p].at[sem], precv[p].at[sem], hop2[p](d))

    def behind(p, axis, d):
        count = (FIRST, SECOND)[axis][p]
        return ((here1, here2)[axis][p] + count - d) % count

    for p in range(3):
        for d in range(1, FIRST[p]):
            go(ag1(p, d, here2[p] * FIRST[p] + here1[p]))
        if p == 0:
            for d in range(1, NZ):
                go(rcopy(tgb.at[loop], tgb.at[loop], tsend.at[d - 1], trecv.at[d - 1], along_z(d)))

    for copy in own:
        copy.wait()

    quarter = HALF // 2
    halves = (pl.ds(0, quarter), pl.ds(quarter, quarter))
    rings = ((0, 4, up, 12), (1, 5, down, 13))

    def ring(n, source, target, half, device):
        return rcopy(
            cbuf.at[source, halves[half]], cbuf.at[target, halves[half]],
            ring_send.at[n], unit_recv.at[2 * target + half], device,
        )

    def whole(n, source, target, device=sibling):
        return rcopy(cbuf.at[source], cbuf.at[target], ring_send.at[n], unit_recv.at[2 * target], device)

    for half in range(2):
        for n, (source, target, device, _) in enumerate(rings):
            go(ring(2 * half + n, source, target, half, device))
    go(whole(4, 0, 2))
    go(whole(5, 1, 3))
    go(whole(6, 1, 6, up))
    go(whole(7, 0, 7, down))

    for p in range(3):
        for d in range(1, FIRST[p]):
            ag1(p, d, here2[p] * FIRST[p] + behind(p, 0, d)).wait_recv()
        for d in range(1, SECOND[p]):
            go(ag2(p, d, here2[p]))
        if p == 0:
            for d in range(1, NZ):
                slot = tgb.at[x * NZ + (z + NZ - d) % NZ]
                rcopy(slot, slot, tsend.at[d - 1], trecv.at[d - 1], along_z(d)).wait_recv()
            for d in range(1, NX):
                line = tgb.at[pl.ds(x * NZ, NZ)]
                sem = NZ - 2 + d
                go(rcopy(line, line, tsend.at[sem], trecv.at[sem], along_x(d)))

    def arrive(*units):
        for u in units:
            whole(0, u, u).wait_recv()

    def rows_of(p):
        for d in range(1, SECOND[p]):
            ag2(p, d, behind(p, 1, d)).wait_recv()
        sbf[p * PART : (p + 1) * PART, :] = joined(ag[p][...].astype(F32)).astype(BF16)

    eye = lax.broadcasted_iota(jnp.int32, (OWN, 128), 0) == lax.broadcasted_iota(jnp.int32, (OWN, 128), 1)
    lanes = lax.broadcasted_iota(jnp.int32, (1, 128), 1)
    block16 = lax.broadcasted_iota(jnp.int32, (8, 128), 1) // 16

    def pick(pieces, first=False):
        rows = pl.ds(0, ROWS)
        cb = jnp.concatenate([cbuf[u, at : at + size] for u, at, size, _ in pieces], axis=0)
        hits = []
        for _, _, size, base in pieces:
            where = tcol[rows, :] - base
            for k in range(size // 128):
                hits.append(jnp.where(where == lanes + k * 128, 1.0, 0.0).astype(BF16))
        hit = jnp.dot(jnp.concatenate(hits, axis=1), cb, preferred_element_type=F32)
        t[rows, :] = hit if first else t[rows, :] + hit

    def chunk(pieces, first=False, picks=True):
        rows = pl.ds(0, ROWS)
        cb = jnp.concatenate([cbuf[u, at : at + size] for u, at, size, _ in pieces], axis=0)
        logits = lax.dot_general(sbf[rows, :], cb, (((1,), (1,)), ((), ())), preferred_element_type=F32)
        new = jnp.max(logits, axis=1, keepdims=True)
        if first:
            new = jnp.broadcast_to(new, (ROWS, 128))
            total = jnp.zeros((ROWS, 128), F32)
        else:
            old = m[rows, :]
            new = jnp.maximum(old, new)
            fade = jnp.exp(old - new)
            total = l[rows, :] * fade
        m[rows, :] = new
        weights = []
        for k in range(cb.shape[0] // 128):
            w = jnp.exp(logits[:, k * 128 : (k + 1) * 128] - new)
            total = total + w
            weights.append(w.astype(BF16))
        l[rows, :] = total
        mean = jnp.dot(jnp.concatenate(weights, axis=1), cb, preferred_element_type=F32)
        if first:
            acc[rows, :] = mean
        else:
            acc[rows, :] = acc[rows, :] * jnp.concatenate([fade, fade], axis=1) + mean
        if picks:
            pick(pieces, first)

    def piece(u, dy, c, h, half=None):
        base = (loop * 2 * NY + ((y + dy) % NY) * 2 + c) * (2 * HALF) + h * HALF
        return (u, 0, HALF, base) if half is None else (u, half * quarter, quarter, base + half * quarter)

    quads = [
        [piece(0, 0, core, 0), piece(1, 0, core, 1), piece(2, 0, other, 0), piece(3, 0, other, 1)],
        [piece(4, 3, core, 0), piece(5, 1, core, 1), piece(6, 3, core, 1), piece(7, 1, core, 0)],
        [piece(8, 3, other, 0), piece(9, 1, other, 1), piece(10, 3, other, 1), piece(11, 1, other, 0)],
    ]
    ends = [
        [piece(12, 2, core, 0, k), piece(13, 2, core, 1, k), piece(14, 2, other, 0, k), piece(15, 2, other, 1, k)]
        for k in range(2)
    ]

    def rs2(p, d, place, which):
        n1 = FIRST[p]
        sem = n1 + SECOND[p] - 3 + d
        make = [
            lambda: rcopy(
                pk[p].at[pl.ds(place * n1, n1)], rx[p].at[d - 1],
                psend[p].at[sem], precv[p].at[sem], hop2[p](d),
            ),
            lambda: rcopy(
                ht[p].at[pl.ds(place * n1, n1)], rht[p].at[d - 1],
                hsend[p].at[d - 1], hrecv[p].at[d - 1], hop2[p](d),
            ),
            lambda: rcopy(
                ls[p].at[place], rls[p].at[d - 1],
                psend[p].at[sem + SECOND[p] - 1], precv[p].at[sem + SECOND[p] - 1], hop2[p](d),
            ),
        ]
        return make[which]()

    def rs1(p, d, place):
        n1 = FIRST[p]
        sem = n1 + 3 * SECOND[p] - 5 + d
        return [
            rcopy(q[p].at[place], rz[p].at[d - 1], psend[p].at[sem], precv[p].at[sem], hop1[p](d)),
            rcopy(qls[p], fls[p].at[d - 1], psend[p].at[sem + n1 - 1], precv[p].at[sem + n1 - 1], hop1[p](d)),
        ]

    def send_picks(p):
        ht[p][...] = parted(t[p * PART : (p + 1) * PART, :]).astype(BF16)
        for d in range(1, SECOND[p]):
            go(rs2(p, d, (here2[p] + d) % SECOND[p], 1))

    def send_part(p):
        n1, n2 = FIRST[p], SECOND[p]
        rows = pl.ds(p * PART, PART)
        total = jnp.sum(l[rows, :], axis=1, keepdims=True)
        l[rows, :] = m[rows, :] + jnp.log(total)
        pk[p][...] = parted(acc[rows, :] * (1.0 / total)).astype(BF16)
        for k in range(n2):
            out = jnp.zeros((8, 128), F32)
            for j in range(n1):
                at = p * PART + 8 * (k * n1 + j)
                out = jnp.where(block16 == j, l[at : at + 8, :], out)
            ls[p][k] = out
        for d in range(1, n2):
            go(rs2(p, d, (here2[p] + d) % n2, 0))
            go(rs2(p, d, (here2[p] + d) % n2, 2))

    def merge_part(p):
        n1, n2 = FIRST[p], SECOND[p]
        for d in range(1, n2):
            for which in range(3):
                rs2(p, d, here2[p], which).wait_recv()
        lse, parts = shares([ls[p][here2[p]]] + [rls[p][d - 1] for d in range(1, n2)])
        qls[p][...] = lse
        for k in range(n1):
            got = [pk[p][here2[p] * n1 + k]] + [rx[p][d - 1, k] for d in range(1, n2)]
            mean = jnp.zeros((16, 128), F32)
            for part, tile in zip(parts, got):
                mean = mean + twice(part[:, 16 * k : 16 * k + 1]) * tile.astype(F32)
            q[p][k, 0] = mean.astype(BF16)
        hit = ht[p][pl.ds(here2[p] * n1, n1)]
        for d in range(1, n2):
            hit = hit + rht[p][d - 1]
        q[p][:, 1] = hit
        for d in range(1, n1):
            for copy in rs1(p, d, (here1[p] + d) % n1):
                go(copy)

    lane8 = lax.broadcasted_iota(jnp.int32, (8, 128), 1)

    def finish_part(p):
        n1 = FIRST[p]
        for d in range(1, n1):
            for copy in rs1(p, d, here1[p]):
                copy.wait_recv()
        lse, parts = shares([qls[p][...]] + [fls[p][d - 1] for d in range(1, n1)])

        def picked_lane(value):
            return jnp.sum(jnp.where(lane8 == 16 * here1[p], value, 0.0), axis=1, keepdims=True)

        mean = jnp.zeros((16, 128), F32)
        hit = jnp.zeros((16, 128), F32)
        for part, tile in zip(parts, [q[p][here1[p]]] + [rz[p][d - 1] for d in range(1, n1)]):
            mean = mean + twice(picked_lane(part)) * tile[0].astype(F32)
            hit = hit + tile[1].astype(F32)
        wide = [jnp.concatenate([v[:8], v[8:]], axis=1) for v in (mean, hit)]
        return wide + [picked_lane(lse)]

    rows_of(0)
    for d in range(1, NX):
        line = tgb.at[pl.ds(((x + NX - d) % NX) * NZ, NZ)]
        sem = NZ - 2 + d
        rcopy(line, line, tsend.at[sem], trecv.at[sem], along_x(d)).wait_recv()
    for k in range(NL):
        row = tgb[k].astype(F32)
        column = jnp.sum(jnp.where(eye, row, 0.0), axis=1, keepdims=True).astype(jnp.int32)
        for p in range(3):
            slot = (k % NZ) * NX + k // NZ if p == 1 else k
            at = p * PART + 8 * slot
            tcol[at : at + 8, :] = jnp.broadcast_to(column[8 * TILE[p] : 8 * TILE[p] + 8], (8, 128))
    def pass_on(half):
        for n, (_, target, device, last) in enumerate(rings):
            ring(0, target, target, half, device).wait_recv()
            go(ring(8 + 2 * half + n, target, last, half, device))

    rows_of(1)
    rows_of(2)
    pass_on(0)
    arrive(2, 3)
    chunk(quads[0], True)
    pass_on(1)
    go(whole(12, 4, 8))
    go(whole(13, 5, 9))
    arrive(6, 7)
    go(whole(14, 6, 10))
    go(whole(15, 7, 11))
    chunk(quads[1])
    for half in range(2):
        for u in (12, 13):
            ring(0, u, u, half, sibling).wait_recv()
            go(ring(4 + 2 * half + u, u, u + 2, half, sibling))
        if half == 0:
            arrive(8, 9, 10, 11)
            chunk(quads[2])
    for half in range(2):
        for u in (14, 15):
            ring(0, u, u, half, sibling).wait_recv()
        if half == 0:
            chunk(ends[0])
    pick(ends[1])
    for p in range(3):
        send_picks(p)
    chunk(ends[1], False, False)
    for p in (0, 2, 1):
        send_part(p)
    merge_part(0)
    merge_part(2)
    merge_part(1)
    done = [finish_part(0), finish_part(1), finish_part(2)]
    mean, hit, lse = [jnp.concatenate([done[0][n], done[2][n], done[1][n]], axis=0) for n in range(3)]
    squashed = jnp.tanh(feats[...].astype(F32) / scale)
    student = (scale * squashed).astype(BF16).astype(F32)
    grad_out[...] = (mean - hit) * (1.0 - squashed * squashed)
    column = lse - jnp.sum(student * hit, axis=1, keepdims=True)
    loss_out[...] = jnp.sum(jnp.where(eye, column, 0.0), axis=0, keepdims=True)

    for copy in sends:
        copy.wait_send()


def body(features, scale_exponents, targets, centres):
    def dma(*shape):
        return pltpu.SemaphoreType.DMA(shape)

    def per_part(make):
        return [make(FIRST[p], SECOND[p]) for p in range(3)]

    loss, grad = pl.pallas_call(
        kernel,
        out_shape=(jax.ShapeDtypeStruct((1, 128), F32), jax.ShapeDtypeStruct((OWN, D), F32)),
        in_specs=[pl.BlockSpec(memory_space=pl.ANY)] * 4,
        out_specs=(pl.BlockSpec(memory_space=pltpu.VMEM), pl.BlockSpec(memory_space=pltpu.VMEM)),
        scratch_shapes=[
            pltpu.SMEM((D // QB,), jnp.int32),
            pltpu.SMEM((OWN,), jnp.int32),
            pltpu.VMEM((OWN, D), BF16),
            pltpu.VMEM((UNITS, HALF, D), BF16),
            pltpu.VMEM((NL, 1, 128), jnp.int32),
            pltpu.VMEM((ROWS, D), BF16),
            pltpu.VMEM((ROWS, 128), jnp.int32),
            pltpu.VMEM((ROWS, 128), F32),
            pltpu.VMEM((ROWS, 128), F32),
            pltpu.VMEM((ROWS, D), F32),
            pltpu.VMEM((ROWS, D), F32),
            *per_part(lambda a, b: pltpu.VMEM((NL, 16, 128), BF16)),
            *per_part(lambda a, b: pltpu.VMEM((NL, 16, 128), BF16)),
            *per_part(lambda a, b: pltpu.VMEM((NL, 16, 128), BF16)),
            *per_part(lambda a, b: pltpu.VMEM((b, 8, 128), F32)),
            *per_part(lambda a, b: pltpu.VMEM((b - 1, a, 16, 128), BF16)),
            *per_part(lambda a, b: pltpu.VMEM((b - 1, a, 16, 128), BF16)),
            *per_part(lambda a, b: pltpu.VMEM((b - 1, 8, 128), F32)),
            *per_part(lambda a, b: pltpu.VMEM((a, 2, 16, 128), BF16)),
            *per_part(lambda a, b: pltpu.VMEM((8, 128), F32)),
            *per_part(lambda a, b: pltpu.VMEM((a - 1, 2, 16, 128), BF16)),
            *per_part(lambda a, b: pltpu.VMEM((a - 1, 8, 128), F32)),
            *per_part(lambda a, b: dma(3 * (a + b - 2))),
            *per_part(lambda a, b: dma(3 * (a + b - 2))),
            *per_part(lambda a, b: dma(b - 1)),
            *per_part(lambda a, b: dma(b - 1)),
            dma(3),
            dma(2),
            dma(20),
            dma(2 * UNITS),
            dma(NX + NZ - 2),
            dma(NX + NZ - 2),
        ],
        compiler_params=pltpu.CompilerParams(
            collective_id=0, has_side_effects=True, vmem_limit_bytes=60 * 1024 * 1024
        ),
    )(scale_exponents, targets, features, centres)
    return loss[0, :OWN], grad


def solution(mesh):
    placed = (P(("loop", "group"), None), P(), P(("loop", "group")), P(("loop", "group"), None))
    return jax.shard_map(
        body,
        mesh=mesh,
        in_specs=placed,
        out_specs=(P(("loop", "group")), P(("loop", "group"), None)),
        check_vma=False,
    )
```

```python
import jax
import jax.numpy as jnp
from jax import lax
from jax.experimental import pallas as pl
from jax.experimental.pallas import tpu as pltpu
from jax.sharding import PartitionSpec as P

F32 = jnp.float32
BF16 = jnp.bfloat16
MESH = pl.DeviceIdType.MESH

NX, NY, NZ = 4, 4, 8
NL = NX * NZ
D = 256
QB = 32
OWN = 24
ROWS = OWN * NL
HALF = 512
UNITS = 16
PART = 8 * NL
FIRST, SECOND = (NZ, NX, NZ), (NX, NZ, NX)
TILE = (0, 2, 1)


def rcopy(src, dst, send, recv, device):
    return pltpu.make_async_remote_copy(
        src_ref=src, dst_ref=dst, send_sem=send, recv_sem=recv, device_id=device, device_id_type=MESH
    )


def joined(tiles):
    count = tiles.shape[0]
    low = tiles[:, :8].reshape(count * 8, 128)
    high = tiles[:, 8:].reshape(count * 8, 128)
    return jnp.concatenate([low, high], axis=1)


def parted(rows):
    count = rows.shape[0] // 8
    low = rows[:, :128].reshape(count, 8, 128)
    high = rows[:, 128:].reshape(count, 8, 128)
    return jnp.concatenate([low, high], axis=1)


def shares(parts):
    top = parts[0]
    for part in parts[1:]:
        top = jnp.maximum(top, part)
    powers = [jnp.exp(part - top) for part in parts]
    total = powers[0]
    for power in powers[1:]:
        total = total + power
    return top + jnp.log(total), [power / total for power in powers]


def twice(column):
    wide = jnp.broadcast_to(column, (8, 128))
    return jnp.concatenate([wide, wide], axis=0)


def kernel(
    exps_hbm, tgts_hbm, feats_hbm, cents, loss_out, grad_out,
    exps, tgts, feats, cbuf, tgb, sbf, tcol, m, l, acc, t, *rest
):
    rest = list(rest)

    def take(count):
        out, rest[:count] = rest[:count], []
        return out

    ag, pk, ht, ls, rx, rht, rls, q, qh, qls, rz, rzh, fls, psend, precv, hsend, hrecv, fsend, frecv = [take(3) for _ in range(19)]
    in_sem, c_sem, ring_send, unit_recv, tsend, trecv = rest
    loop = lax.axis_index("loop")
    group = lax.axis_index("group")
    x, z = loop // NZ, loop % NZ
    y, core = group // 2, group % 2
    other = 1 - core

    def chip(dx, dy, c):
        return (((x + dx + NX) % NX) * NZ + z, ((y + dy + NY) % NY) * 2 + c)

    def along_x(d):
        return chip(d, 0, core)

    def along_z(d):
        return (x * NZ + (z + d) % NZ, group)

    sibling = chip(0, 0, other)
    up, down = chip(0, 1, core), chip(0, -1, core)
    barrier = pltpu.get_barrier_semaphore()
    partners = [along_z(d) for d in range(1, NZ)] + [along_x(d) for d in range(1, NX)]
    partners += [sibling, up, down]
    for partner in partners:
        pl.semaphore_signal(barrier, inc=1, device_id=partner, device_id_type=MESH)

    small = [
        pltpu.make_async_copy(exps_hbm, exps, in_sem.at[0]),
        pltpu.make_async_copy(tgts_hbm, tgts, in_sem.at[1]),
        pltpu.make_async_copy(feats_hbm, feats, in_sem.at[2]),
    ]
    own = [
        pltpu.make_async_copy(cents.at[pl.ds(h * HALF, HALF)], cbuf.at[h], c_sem.at[h]) for h in range(2)
    ]
    for copy in small + own:
        copy.start()
    for copy in small:
        copy.wait()

    hop1 = (along_z, along_x, along_z)
    hop2 = (along_x, along_z, along_x)
    here1, here2 = (z, x, z), (x, z, x)

    block = lax.broadcasted_iota(jnp.int32, (1, D), 1) // QB
    scale = jnp.zeros((1, D), F32)
    for b in range(D // QB):
        e = exps[b]
        power = jnp.where(e < 0, 0.5, jnp.where(e < 1, 1.0, jnp.where(e < 2, 2.0, 4.0)))
        scale = jnp.where(block == b, power, scale)
    squashed = jnp.tanh(feats[...].astype(F32) / scale)
    student = (scale * squashed).astype(BF16).astype(F32)
    tiles = parted(student).astype(BF16)
    for p in range(3):
        ag[p][here2[p] * FIRST[p] + here1[p]] = tiles[TILE[p]]
    lane = lax.broadcasted_iota(jnp.int32, (1, 128), 1)
    ids = jnp.zeros((1, 128), jnp.int32)
    for i in range(OWN):
        ids = jnp.where(lane == i, tgts[i], ids)
    tgb[loop] = ids

    pl.semaphore_wait(barrier, len(partners))

    sends = []

    def go(copy):
        copy.start()
        sends.append(copy)

    def ag1(p, d, slot):
        ref = ag[p].at[slot]
        return rcopy(ref, ref, psend[p].at[d - 1], precv[p].at[d - 1], hop1[p](d))

    def ag2(p, d, place):
        ref = ag[p].at[pl.ds(place * FIRST[p], FIRST[p])]
        sem = FIRST[p] - 2 + d
        return rcopy(ref, ref, psend[p].at[sem], precv[p].at[sem], hop2[p](d))

    def behind(p, axis, d):
        count = (FIRST, SECOND)[axis][p]
        return ((here1, here2)[axis][p] + count - d) % count

    for p in range(3):
        for d in range(1, FIRST[p]):
            go(ag1(p, d, here2[p] * FIRST[p] + here1[p]))
        if p == 0:
            for d in range(1, NZ):
                go(rcopy(tgb.at[loop], tgb.at[loop], tsend.at[d - 1], trecv.at[d - 1], along_z(d)))

    for copy in own:
        copy.wait()

    quarter = HALF // 2
    halves = (pl.ds(0, quarter), pl.ds(quarter, quarter))
    rings = ((0, 4, up, 12), (1, 5, down, 13))

    def ring(n, source, target, half, device):
        return rcopy(
            cbuf.at[source, halves[half]], cbuf.at[target, halves[half]],
            ring_send.at[n], unit_recv.at[2 * target + half], device,
        )

    def whole(n, source, target, device=sibling):
        return rcopy(cbuf.at[source], cbuf.at[target], ring_send.at[n], unit_recv.at[2 * target], device)

    for half in range(2):
        for n, (source, target, device, _) in enumerate(rings):
            go(ring(2 * half + n, source, target, half, device))
    go(whole(4, 0, 2))
    go(whole(5, 1, 3))
    go(whole(6, 1, 6, up))
    go(whole(7, 0, 7, down))

    for p in range(3):
        for d in range(1, FIRST[p]):
            ag1(p, d, here2[p] * FIRST[p] + behind(p, 0, d)).wait_recv()
        for d in range(1, SECOND[p]):
            go(ag2(p, d, here2[p]))
        if p == 0:
            for d in range(1, NZ):
                slot = tgb.at[x * NZ + (z + NZ - d) % NZ]
                rcopy(slot, slot, tsend.at[d - 1], trecv.at[d - 1], along_z(d)).wait_recv()
            for d in range(1, NX):
                line = tgb.at[pl.ds(x * NZ, NZ)]
                sem = NZ - 2 + d
                go(rcopy(line, line, tsend.at[sem], trecv.at[sem], along_x(d)))

    def arrive(*units):
        for u in units:
            whole(0, u, u).wait_recv()

    def rows_of(p):
        for d in range(1, SECOND[p]):
            ag2(p, d, behind(p, 1, d)).wait_recv()
        sbf[p * PART : (p + 1) * PART, :] = joined(ag[p][...].astype(F32)).astype(BF16)

    eye = lax.broadcasted_iota(jnp.int32, (OWN, 128), 0) == lax.broadcasted_iota(jnp.int32, (OWN, 128), 1)
    lanes = lax.broadcasted_iota(jnp.int32, (1, 128), 1)
    block8 = lax.broadcasted_iota(jnp.int32, (8, 128), 1) // 8
    shift = (0, 0, NZ)

    def pick(pieces, first=False):
        rows = pl.ds(0, ROWS)
        cb = jnp.concatenate([cbuf[u, at : at + size] for u, at, size, _ in pieces], axis=0)
        hits = []
        for _, _, size, base in pieces:
            where = tcol[rows, :] - base
            for k in range(size // 128):
                hits.append(jnp.where(where == lanes + k * 128, 1.0, 0.0).astype(BF16))
        hit = jnp.dot(jnp.concatenate(hits, axis=1), cb, preferred_element_type=F32)
        t[rows, :] = hit if first else t[rows, :] + hit

    def chunk(pieces, first=False, picks=True):
        rows = pl.ds(0, ROWS)
        cb = jnp.concatenate([cbuf[u, at : at + size] for u, at, size, _ in pieces], axis=0)
        logits = lax.dot_general(sbf[rows, :], cb, (((1,), (1,)), ((), ())), preferred_element_type=F32)
        new = jnp.max(logits, axis=1, keepdims=True)
        if first:
            new = jnp.broadcast_to(new, (ROWS, 128))
            total = jnp.zeros((ROWS, 128), F32)
        else:
            old = m[rows, :]
            new = jnp.maximum(old, new)
            fade = jnp.exp(old - new)
            total = l[rows, :] * fade
        m[rows, :] = new
        weights = []
        for k in range(cb.shape[0] // 128):
            w = jnp.exp(logits[:, k * 128 : (k + 1) * 128] - new)
            total = total + w
            weights.append(w.astype(BF16))
        l[rows, :] = total
        mean = jnp.dot(jnp.concatenate(weights, axis=1), cb, preferred_element_type=F32)
        if first:
            acc[rows, :] = mean
        else:
            acc[rows, :] = acc[rows, :] * jnp.concatenate([fade, fade], axis=1) + mean
        if picks:
            pick(pieces, first)

    def piece(u, dy, c, h, half=None):
        base = (loop * 2 * NY + ((y + dy) % NY) * 2 + c) * (2 * HALF) + h * HALF
        return (u, 0, HALF, base) if half is None else (u, half * quarter, quarter, base + half * quarter)

    quads = [
        [piece(0, 0, core, 0), piece(1, 0, core, 1), piece(2, 0, other, 0), piece(3, 0, other, 1)],
        [piece(4, 3, core, 0), piece(5, 1, core, 1), piece(6, 3, core, 1), piece(7, 1, core, 0)],
        [piece(8, 3, other, 0), piece(9, 1, other, 1), piece(10, 3, other, 1), piece(11, 1, other, 0)],
    ]
    ends = [
        [piece(12, 2, core, 0, k), piece(13, 2, core, 1, k), piece(14, 2, other, 0, k), piece(15, 2, other, 1, k)]
        for k in range(2)
    ]

    def rs2(p, d, place, which):
        n1 = FIRST[p]
        sem = n1 + SECOND[p] - 3 + d
        make = [
            lambda: rcopy(
                pk[p].at[pl.ds(place * n1, n1)], rx[p].at[d - 1],
                psend[p].at[sem], precv[p].at[sem], hop2[p](d),
            ),
            lambda: rcopy(
                ht[p].at[pl.ds(place * n1, n1)], rht[p].at[d - 1],
                hsend[p].at[d - 1], hrecv[p].at[d - 1], hop2[p](d),
            ),
            lambda: rcopy(
                ls[p].at[place], rls[p].at[d - 1],
                psend[p].at[sem + SECOND[p] - 1], precv[p].at[sem + SECOND[p] - 1], hop2[p](d),
            ),
        ]
        return make[which]()

    def rs1(p, d, place, which):
        n1 = FIRST[p]
        sem = n1 + 3 * SECOND[p] - 5 + d
        far = sem + n1 - 1
        make = [
            lambda: rcopy(q[p].at[place], rz[p].at[d - 1], psend[p].at[sem], precv[p].at[sem], hop1[p](d)),
            lambda: rcopy(qh[p].at[place], rzh[p].at[d - 1], fsend[p].at[d - 1], frecv[p].at[d - 1], hop1[p](d)),
            lambda: rcopy(qls[p], fls[p].at[d - 1], psend[p].at[far], precv[p].at[far], hop1[p](d)),
        ]
        return make[which]()

    def send_picks(p):
        ht[p][...] = parted(t[p * PART : (p + 1) * PART, :]).astype(BF16)
        for d in range(1, SECOND[p]):
            go(rs2(p, d, (here2[p] + d) % SECOND[p], 1))

    def send_part(p):
        n1, n2 = FIRST[p], SECOND[p]
        rows = pl.ds(p * PART, PART)
        total = jnp.sum(l[rows, :], axis=1, keepdims=True)
        l[rows, :] = m[rows, :] + jnp.log(total)
        pk[p][...] = parted(acc[rows, :] * (1.0 / total)).astype(BF16)
        for k in range(n2):
            out = jnp.zeros((8, 128), F32)
            for j in range(n1):
                at = p * PART + 8 * (k * n1 + j)
                out = jnp.where(block8 == shift[p] + j, l[at : at + 8, :], out)
            ls[p][k] = out
        for d in range(1, n2):
            go(rs2(p, d, (here2[p] + d) % n2, 0))
            go(rs2(p, d, (here2[p] + d) % n2, 2))

    def merge_picks(p):
        n1, n2 = FIRST[p], SECOND[p]
        for d in range(1, n2):
            rs2(p, d, here2[p], 1).wait_recv()
        hit = ht[p][pl.ds(here2[p] * n1, n1)]
        for d in range(1, n2):
            hit = hit + rht[p][d - 1]
        qh[p][...] = hit
        for d in range(1, n1):
            go(rs1(p, d, (here1[p] + d) % n1, 1))

    def merge_part(p):
        n1, n2 = FIRST[p], SECOND[p]
        for d in range(1, n2):
            rs2(p, d, here2[p], 0).wait_recv()
            rs2(p, d, here2[p], 2).wait_recv()
        lse, parts = shares([ls[p][here2[p]]] + [rls[p][d - 1] for d in range(1, n2)])
        qls[p][...] = jnp.where(block8 < NZ, qls[0][...], lse) if p == 2 else lse
        for k in range(n1):
            got = [pk[p][here2[p] * n1 + k]] + [rx[p][d - 1, k] for d in range(1, n2)]
            mean = jnp.zeros((16, 128), F32)
            for part, tile in zip(parts, got):
                at = 8 * (shift[p] + k)
                mean = mean + twice(part[:, at : at + 1]) * tile.astype(F32)
            q[p][k] = mean.astype(BF16)
        for d in range(1, n1):
            go(rs1(p, d, (here1[p] + d) % n1, 0))
            if p != 0:
                go(rs1(p, d, (here1[p] + d) % n1, 2))

    lane8 = lax.broadcasted_iota(jnp.int32, (8, 128), 1)

    def finish_part(p, lse, parts):
        n1 = FIRST[p]
        for d in range(1, n1):
            rs1(p, d, here1[p], 0).wait_recv()
            rs1(p, d, here1[p], 1).wait_recv()

        def picked_lane(value):
            return jnp.sum(jnp.where(lane8 == 8 * (shift[p] + here1[p]), value, 0.0), axis=1, keepdims=True)

        mean = jnp.zeros((16, 128), F32)
        for part, tile in zip(parts, [q[p][here1[p]]] + [rz[p][d - 1] for d in range(1, n1)]):
            mean = mean + twice(picked_lane(part)) * tile.astype(F32)
        hit = qh[p][here1[p]]
        for d in range(1, n1):
            hit = hit + rzh[p][d - 1]
        wide = [jnp.concatenate([v[:8], v[8:]], axis=1) for v in (mean, hit.astype(F32))]
        return wide + [picked_lane(lse)]

    def last_shares(p):
        for d in range(1, FIRST[p]):
            rs1(p, d, here1[p], 2).wait_recv()
        return shares([qls[p][...]] + [fls[p][d - 1] for d in range(1, FIRST[p])])

    rows_of(0)
    for d in range(1, NX):
        line = tgb.at[pl.ds(((x + NX - d) % NX) * NZ, NZ)]
        sem = NZ - 2 + d
        rcopy(line, line, tsend.at[sem], trecv.at[sem], along_x(d)).wait_recv()
    for k in range(NL):
        row = tgb[k].astype(F32)
        column = jnp.sum(jnp.where(eye, row, 0.0), axis=1, keepdims=True).astype(jnp.int32)
        for p in range(3):
            slot = (k % NZ) * NX + k // NZ if p == 1 else k
            at = p * PART + 8 * slot
            tcol[at : at + 8, :] = jnp.broadcast_to(column[8 * TILE[p] : 8 * TILE[p] + 8], (8, 128))
    def pass_on(half):
        for n, (_, target, device, last) in enumerate(rings):
            ring(0, target, target, half, device).wait_recv()
            go(ring(8 + 2 * half + n, target, last, half, device))

    rows_of(1)
    rows_of(2)
    pass_on(0)
    arrive(2, 3)
    chunk(quads[0], True)
    pass_on(1)
    go(whole(12, 4, 8))
    go(whole(13, 5, 9))
    arrive(6, 7)
    go(whole(14, 6, 10))
    go(whole(15, 7, 11))
    chunk(quads[1])
    for half in range(2):
        for u in (12, 13):
            ring(0, u, u, half, sibling).wait_recv()
            go(ring(4 + 2 * half + u, u, u + 2, half, sibling))
        if half == 0:
            arrive(8, 9, 10, 11)
            chunk(quads[2])
    for half in range(2):
        for u in (14, 15):
            ring(0, u, u, half, sibling).wait_recv()
        if half == 0:
            chunk(ends[0])
    pick(ends[1])
    early = list(sends)
    sends.clear()
    for p in range(3):
        send_picks(p)
    chunk(ends[1], False, False)
    for p in (0, 2, 1):
        send_part(p)
    for copy in early:
        copy.wait_send()
    for p in (0, 2, 1):
        merge_picks(p)
    for p in (0, 2, 1):
        merge_part(p)
    both = last_shares(2)
    done = [finish_part(0, *both), finish_part(1, *last_shares(1)), finish_part(2, *both)]
    mean, hit, lse = [jnp.concatenate([done[0][n], done[2][n], done[1][n]], axis=0) for n in range(3)]
    squashed = jnp.tanh(feats[...].astype(F32) / scale)
    student = (scale * squashed).astype(BF16).astype(F32)
    grad_out[...] = (mean - hit) * (1.0 - squashed * squashed)
    column = lse - jnp.sum(student * hit, axis=1, keepdims=True)
    loss_out[...] = jnp.sum(jnp.where(eye, column, 0.0), axis=0, keepdims=True)

    for copy in sends:
        copy.wait_send()


def body(features, scale_exponents, targets, centres):
    def dma(*shape):
        return pltpu.SemaphoreType.DMA(shape)

    def per_part(make):
        return [make(FIRST[p], SECOND[p]) for p in range(3)]

    loss, grad = pl.pallas_call(
        kernel,
        out_shape=(jax.ShapeDtypeStruct((1, 128), F32), jax.ShapeDtypeStruct((OWN, D), F32)),
        in_specs=[pl.BlockSpec(memory_space=pl.ANY)] * 4,
        out_specs=(pl.BlockSpec(memory_space=pltpu.VMEM), pl.BlockSpec(memory_space=pltpu.VMEM)),
        scratch_shapes=[
            pltpu.SMEM((D // QB,), jnp.int32),
            pltpu.SMEM((OWN,), jnp.int32),
            pltpu.VMEM((OWN, D), BF16),
            pltpu.VMEM((UNITS, HALF, D), BF16),
            pltpu.VMEM((NL, 1, 128), jnp.int32),
            pltpu.VMEM((ROWS, D), BF16),
            pltpu.VMEM((ROWS, 128), jnp.int32),
            pltpu.VMEM((ROWS, 128), F32),
            pltpu.VMEM((ROWS, 128), F32),
            pltpu.VMEM((ROWS, D), F32),
            pltpu.VMEM((ROWS, D), F32),
            *per_part(lambda a, b: pltpu.VMEM((NL, 16, 128), BF16)),
            *per_part(lambda a, b: pltpu.VMEM((NL, 16, 128), BF16)),
            *per_part(lambda a, b: pltpu.VMEM((NL, 16, 128), BF16)),
            *per_part(lambda a, b: pltpu.VMEM((b, 8, 128), F32)),
            *per_part(lambda a, b: pltpu.VMEM((b - 1, a, 16, 128), BF16)),
            *per_part(lambda a, b: pltpu.VMEM((b - 1, a, 16, 128), BF16)),
            *per_part(lambda a, b: pltpu.VMEM((b - 1, 8, 128), F32)),
            *per_part(lambda a, b: pltpu.VMEM((a, 16, 128), BF16)),
            *per_part(lambda a, b: pltpu.VMEM((a, 16, 128), BF16)),
            *per_part(lambda a, b: pltpu.VMEM((8, 128), F32)),
            *per_part(lambda a, b: pltpu.VMEM((a - 1, 16, 128), BF16)),
            *per_part(lambda a, b: pltpu.VMEM((a - 1, 16, 128), BF16)),
            *per_part(lambda a, b: pltpu.VMEM((a - 1, 8, 128), F32)),
            *per_part(lambda a, b: dma(3 * (a + b - 2))),
            *per_part(lambda a, b: dma(3 * (a + b - 2))),
            *per_part(lambda a, b: dma(b - 1)),
            *per_part(lambda a, b: dma(b - 1)),
            *per_part(lambda a, b: dma(a - 1)),
            *per_part(lambda a, b: dma(a - 1)),
            dma(3),
            dma(2),
            dma(20),
            dma(2 * UNITS),
            dma(NX + NZ - 2),
            dma(NX + NZ - 2),
        ],
        compiler_params=pltpu.CompilerParams(
            collective_id=0, has_side_effects=True, vmem_limit_bytes=60 * 1024 * 1024
        ),
    )(scale_exponents, targets, features, centres)
    return loss[0, :OWN], grad


def solution(mesh):
    placed = (P(("loop", "group"), None), P(), P(("loop", "group")), P(("loop", "group"), None))
    return jax.shard_map(
        body,
        mesh=mesh,
        in_specs=placed,
        out_specs=(P(("loop", "group")), P(("loop", "group"), None)),
        check_vma=False,
    )
```

```python
import jax
import jax.numpy as jnp
from jax import lax
from jax.experimental import pallas as pl
from jax.experimental.pallas import tpu as pltpu
from jax.sharding import PartitionSpec as P

F32 = jnp.float32
BF16 = jnp.bfloat16
MESH = pl.DeviceIdType.MESH

NX, NY, NZ = 4, 4, 8
NL = NX * NZ
D = 256
QB = 32
OWN = 24
ROWS = OWN * NL
HALF = 512
UNITS = 16
PART = 8 * NL
FIRST, SECOND = (NZ, NX, NZ), (NX, NZ, NX)
TILE = (0, 2, 1)


def rcopy(src, dst, send, recv, device):
    return pltpu.make_async_remote_copy(
        src_ref=src, dst_ref=dst, send_sem=send, recv_sem=recv, device_id=device, device_id_type=MESH
    )


def joined(tiles):
    count = tiles.shape[0]
    low = tiles[:, :8].reshape(count * 8, 128)
    high = tiles[:, 8:].reshape(count * 8, 128)
    return jnp.concatenate([low, high], axis=1)


def parted(rows):
    count = rows.shape[0] // 8
    low = rows[:, :128].reshape(count, 8, 128)
    high = rows[:, 128:].reshape(count, 8, 128)
    return jnp.concatenate([low, high], axis=1)


def shares(parts):
    top = parts[0]
    for part in parts[1:]:
        top = jnp.maximum(top, part)
    powers = [jnp.exp(part - top) for part in parts]
    total = powers[0]
    for power in powers[1:]:
        total = total + power
    return top + jnp.log(total), [power / total for power in powers]


def twice(column):
    wide = jnp.broadcast_to(column, (8, 128))
    return jnp.concatenate([wide, wide], axis=0)


def kernel(
    exps_hbm, tgts_hbm, feats_hbm, cents, loss_out, grad_out,
    exps, tgts, feats, cbuf, tgb, sbf, tcol, m, l, acc, t, *rest
):
    rest = list(rest)

    def take(count):
        out, rest[:count] = rest[:count], []
        return out

    ag, pk, ht, ls, rx, rht, rls, q, qh, qls, rz, rzh, fls, psend, precv, hsend, hrecv, fsend, frecv = [take(3) for _ in range(19)]
    in_sem, c_sem, ring_send, unit_recv, tsend, trecv = rest
    loop = lax.axis_index("loop")
    group = lax.axis_index("group")
    x, z = loop // NZ, loop % NZ
    y, core = group // 2, group % 2
    other = 1 - core

    def chip(dx, dy, c):
        return (((x + dx + NX) % NX) * NZ + z, ((y + dy + NY) % NY) * 2 + c)

    def along_x(d):
        return chip(d, 0, core)

    def along_z(d):
        return (x * NZ + (z + d) % NZ, group)

    sibling = chip(0, 0, other)
    up, down = chip(0, 1, core), chip(0, -1, core)
    barrier = pltpu.get_barrier_semaphore()
    partners = [along_z(d) for d in range(1, NZ)] + [along_x(d) for d in range(1, NX)]
    partners += [sibling, up, down]
    for partner in partners:
        pl.semaphore_signal(barrier, inc=1, device_id=partner, device_id_type=MESH)

    small = [
        pltpu.make_async_copy(exps_hbm, exps, in_sem.at[0]),
        pltpu.make_async_copy(tgts_hbm, tgts, in_sem.at[1]),
        pltpu.make_async_copy(feats_hbm, feats, in_sem.at[2]),
    ]
    own = [
        pltpu.make_async_copy(cents.at[pl.ds(h * HALF, HALF)], cbuf.at[h], c_sem.at[h]) for h in range(2)
    ]
    for copy in small + own:
        copy.start()
    for copy in small:
        copy.wait()

    hop1 = (along_z, along_x, along_z)
    hop2 = (along_x, along_z, along_x)
    here1, here2 = (z, x, z), (x, z, x)

    block = lax.broadcasted_iota(jnp.int32, (1, D), 1) // QB
    scale = jnp.zeros((1, D), F32)
    for b in range(D // QB):
        e = exps[b]
        power = jnp.where(e < 0, 0.5, jnp.where(e < 1, 1.0, jnp.where(e < 2, 2.0, 4.0)))
        scale = jnp.where(block == b, power, scale)
    squashed = jnp.tanh(feats[...].astype(F32) / scale)
    student = (scale * squashed).astype(BF16).astype(F32)
    tiles = parted(student).astype(BF16)
    for p in range(3):
        ag[p][here2[p] * FIRST[p] + here1[p]] = tiles[TILE[p]]
    lane = lax.broadcasted_iota(jnp.int32, (1, 128), 1)
    ids = jnp.zeros((1, 128), jnp.int32)
    for i in range(OWN):
        ids = jnp.where(lane == i, tgts[i], ids)
    tgb[loop] = ids

    pl.semaphore_wait(barrier, len(partners))

    sends = []

    def go(copy):
        copy.start()
        sends.append(copy)

    def ag1(p, d, slot):
        ref = ag[p].at[slot]
        return rcopy(ref, ref, psend[p].at[d - 1], precv[p].at[d - 1], hop1[p](d))

    def ag2(p, d, place):
        ref = ag[p].at[pl.ds(place * FIRST[p], FIRST[p])]
        sem = FIRST[p] - 2 + d
        return rcopy(ref, ref, psend[p].at[sem], precv[p].at[sem], hop2[p](d))

    def behind(p, axis, d):
        count = (FIRST, SECOND)[axis][p]
        return ((here1, here2)[axis][p] + count - d) % count

    for p in range(3):
        for d in range(1, FIRST[p]):
            go(ag1(p, d, here2[p] * FIRST[p] + here1[p]))
        if p == 0:
            for d in range(1, NZ):
                go(rcopy(tgb.at[loop], tgb.at[loop], tsend.at[d - 1], trecv.at[d - 1], along_z(d)))

    for copy in own:
        copy.wait()

    quarter = HALF // 2
    halves = (pl.ds(0, quarter), pl.ds(quarter, quarter))
    rings = ((0, 4, up, 12), (1, 5, down, 13))

    def ring(n, source, target, half, device):
        return rcopy(
            cbuf.at[source, halves[half]], cbuf.at[target, halves[half]],
            ring_send.at[n], unit_recv.at[2 * target + half], device,
        )

    def whole(n, source, target, device=sibling):
        return rcopy(cbuf.at[source], cbuf.at[target], ring_send.at[n], unit_recv.at[2 * target], device)

    for half in range(2):
        for n, (source, target, device, _) in enumerate(rings):
            go(ring(2 * half + n, source, target, half, device))
    go(whole(4, 0, 2))
    go(whole(5, 1, 3))
    go(whole(6, 1, 6, up))
    go(whole(7, 0, 7, down))

    for p in range(3):
        for d in range(1, FIRST[p]):
            ag1(p, d, here2[p] * FIRST[p] + behind(p, 0, d)).wait_recv()
        for d in range(1, SECOND[p]):
            go(ag2(p, d, here2[p]))
        if p == 0:
            for d in range(1, NZ):
                slot = tgb.at[x * NZ + (z + NZ - d) % NZ]
                rcopy(slot, slot, tsend.at[d - 1], trecv.at[d - 1], along_z(d)).wait_recv()
            for d in range(1, NX):
                line = tgb.at[pl.ds(x * NZ, NZ)]
                sem = NZ - 2 + d
                go(rcopy(line, line, tsend.at[sem], trecv.at[sem], along_x(d)))

    def arrive(*units):
        for u in units:
            whole(0, u, u).wait_recv()

    def rows_of(p):
        for d in range(1, SECOND[p]):
            ag2(p, d, behind(p, 1, d)).wait_recv()
        sbf[p * PART : (p + 1) * PART, :] = joined(ag[p][...].astype(F32)).astype(BF16)

    eye = lax.broadcasted_iota(jnp.int32, (OWN, 128), 0) == lax.broadcasted_iota(jnp.int32, (OWN, 128), 1)
    lanes = lax.broadcasted_iota(jnp.int32, (1, 128), 1)
    block8 = lax.broadcasted_iota(jnp.int32, (8, 128), 1) // 8
    shift = (0, 0, NZ)

    def pick(pieces, first=False):
        rows = pl.ds(0, ROWS)
        cb = jnp.concatenate([cbuf[u, at : at + size] for u, at, size, _ in pieces], axis=0)
        hits = []
        for _, _, size, base in pieces:
            where = tcol[rows, :] - base
            for k in range(size // 128):
                hits.append(jnp.where(where == lanes + k * 128, 1.0, 0.0).astype(BF16))
        hit = jnp.dot(jnp.concatenate(hits, axis=1), cb, preferred_element_type=F32)
        t[rows, :] = hit if first else t[rows, :] + hit

    def chunk(pieces, first=False, picks=True):
        rows = pl.ds(0, ROWS)
        cb = jnp.concatenate([cbuf[u, at : at + size] for u, at, size, _ in pieces], axis=0)
        logits = lax.dot_general(sbf[rows, :], cb, (((1,), (1,)), ((), ())), preferred_element_type=F32)
        new = jnp.max(logits, axis=1, keepdims=True)
        if first:
            new = jnp.broadcast_to(new, (ROWS, 128))
            total = jnp.zeros((ROWS, 128), F32)
        else:
            old = m[rows, :]
            new = jnp.maximum(old, new)
            fade = jnp.exp(old - new)
            total = l[rows, :] * fade
        m[rows, :] = new
        weights = []
        for k in range(cb.shape[0] // 128):
            w = jnp.exp(logits[:, k * 128 : (k + 1) * 128] - new)
            total = total + w
            weights.append(w.astype(BF16))
        l[rows, :] = total
        mean = jnp.dot(jnp.concatenate(weights, axis=1), cb, preferred_element_type=F32)
        if first:
            acc[rows, :] = mean
        else:
            acc[rows, :] = acc[rows, :] * jnp.concatenate([fade, fade], axis=1) + mean
        if picks:
            pick(pieces, first)

    def piece(u, dy, c, h, half=None):
        base = (loop * 2 * NY + ((y + dy) % NY) * 2 + c) * (2 * HALF) + h * HALF
        return (u, 0, HALF, base) if half is None else (u, half * quarter, quarter, base + half * quarter)

    quads = [
        [piece(0, 0, core, 0), piece(1, 0, core, 1), piece(2, 0, other, 0), piece(3, 0, other, 1)],
        [piece(4, 3, core, 0), piece(5, 1, core, 1), piece(6, 3, core, 1), piece(7, 1, core, 0)],
        [piece(8, 3, other, 0), piece(9, 1, other, 1), piece(10, 3, other, 1), piece(11, 1, other, 0)],
    ]
    ends = [
        [piece(12, 2, core, 0, k), piece(13, 2, core, 1, k), piece(14, 2, other, 0, k), piece(15, 2, other, 1, k)]
        for k in range(2)
    ]

    def rs2(p, d, place, which):
        n1 = FIRST[p]
        sem = n1 + SECOND[p] - 3 + d
        make = [
            lambda: rcopy(
                pk[p].at[pl.ds(place * n1, n1)], rx[p].at[d - 1],
                psend[p].at[sem], precv[p].at[sem], hop2[p](d),
            ),
            lambda: rcopy(
                ht[p].at[pl.ds(place * n1, n1)], rht[p].at[d - 1],
                hsend[p].at[d - 1], hrecv[p].at[d - 1], hop2[p](d),
            ),
            lambda: rcopy(
                ls[p].at[place], rls[p].at[d - 1],
                psend[p].at[sem + SECOND[p] - 1], precv[p].at[sem + SECOND[p] - 1], hop2[p](d),
            ),
        ]
        return make[which]()

    def rs1(p, d, place, which):
        n1 = FIRST[p]
        sem = n1 + 3 * SECOND[p] - 5 + d
        far = sem + n1 - 1
        make = [
            lambda: rcopy(q[p].at[place], rz[p].at[d - 1], psend[p].at[sem], precv[p].at[sem], hop1[p](d)),
            lambda: rcopy(qh[p].at[place], rzh[p].at[d - 1], fsend[p].at[d - 1], frecv[p].at[d - 1], hop1[p](d)),
            lambda: rcopy(qls[p], fls[p].at[d - 1], psend[p].at[far], precv[p].at[far], hop1[p](d)),
        ]
        return make[which]()

    def send_picks(p):
        ht[p][...] = parted(t[p * PART : (p + 1) * PART, :]).astype(BF16)
        for d in range(1, SECOND[p]):
            go(rs2(p, d, (here2[p] + d) % SECOND[p], 1))

    def send_part(p):
        n1, n2 = FIRST[p], SECOND[p]
        rows = pl.ds(p * PART, PART)
        total = jnp.sum(l[rows, :], axis=1, keepdims=True)
        l[rows, :] = m[rows, :] + jnp.log(total)
        pk[p][...] = parted(acc[rows, :] * (1.0 / total)).astype(BF16)
        for k in range(n2):
            out = jnp.zeros((8, 128), F32)
            for j in range(n1):
                at = p * PART + 8 * (k * n1 + j)
                out = jnp.where(block8 == shift[p] + j, l[at : at + 8, :], out)
            ls[p][k] = out
        for d in range(1, n2):
            go(rs2(p, d, (here2[p] + d) % n2, 0))
            go(rs2(p, d, (here2[p] + d) % n2, 2))

    def merge_picks(p):
        n1, n2 = FIRST[p], SECOND[p]
        for d in range(1, n2):
            rs2(p, d, here2[p], 1).wait_recv()
        hit = ht[p][pl.ds(here2[p] * n1, n1)]
        for d in range(1, n2):
            hit = hit + rht[p][d - 1]
        qh[p][...] = hit
        for d in range(1, n1):
            go(rs1(p, d, (here1[p] + d) % n1, 1))

    def merge_part(p):
        n1, n2 = FIRST[p], SECOND[p]
        for d in range(1, n2):
            rs2(p, d, here2[p], 0).wait_recv()
            rs2(p, d, here2[p], 2).wait_recv()
        lse, parts = shares([ls[p][here2[p]]] + [rls[p][d - 1] for d in range(1, n2)])
        qls[p][...] = jnp.where(block8 < NZ, qls[0][...], lse) if p == 2 else lse
        for k in range(n1):
            got = [pk[p][here2[p] * n1 + k]] + [rx[p][d - 1, k] for d in range(1, n2)]
            mean = jnp.zeros((16, 128), F32)
            for part, tile in zip(parts, got):
                at = 8 * (shift[p] + k)
                mean = mean + twice(part[:, at : at + 1]) * tile.astype(F32)
            q[p][k] = mean.astype(BF16)
        for d in range(1, n1):
            go(rs1(p, d, (here1[p] + d) % n1, 0))
            if p != 0:
                go(rs1(p, d, (here1[p] + d) % n1, 2))

    lane8 = lax.broadcasted_iota(jnp.int32, (8, 128), 1)

    def finish_part(p, lse, parts):
        n1 = FIRST[p]
        for d in range(1, n1):
            rs1(p, d, here1[p], 0).wait_recv()
            rs1(p, d, here1[p], 1).wait_recv()

        def picked_lane(value):
            return jnp.sum(jnp.where(lane8 == 8 * (shift[p] + here1[p]), value, 0.0), axis=1, keepdims=True)

        mean = jnp.zeros((16, 128), F32)
        for part, tile in zip(parts, [q[p][here1[p]]] + [rz[p][d - 1] for d in range(1, n1)]):
            mean = mean + twice(picked_lane(part)) * tile.astype(F32)
        hit = qh[p][here1[p]]
        for d in range(1, n1):
            hit = hit + rzh[p][d - 1]
        wide = [jnp.concatenate([v[:8], v[8:]], axis=1) for v in (mean, hit.astype(F32))]
        return wide + [picked_lane(lse)]

    def last_shares(p):
        for d in range(1, FIRST[p]):
            rs1(p, d, here1[p], 2).wait_recv()
        return shares([qls[p][...]] + [fls[p][d - 1] for d in range(1, FIRST[p])])

    rows_of(0)
    for d in range(1, NX):
        line = tgb.at[pl.ds(((x + NX - d) % NX) * NZ, NZ)]
        sem = NZ - 2 + d
        rcopy(line, line, tsend.at[sem], trecv.at[sem], along_x(d)).wait_recv()
    for k in range(NL):
        row = tgb[k].astype(F32)
        column = jnp.sum(jnp.where(eye, row, 0.0), axis=1, keepdims=True).astype(jnp.int32)
        for p in range(3):
            slot = (k % NZ) * NX + k // NZ if p == 1 else k
            at = p * PART + 8 * slot
            tcol[at : at + 8, :] = jnp.broadcast_to(column[8 * TILE[p] : 8 * TILE[p] + 8], (8, 128))
    def pass_on(half):
        for n, (_, target, device, last) in enumerate(rings):
            ring(0, target, target, half, device).wait_recv()
            go(ring(8 + 2 * half + n, target, last, half, device))

    rows_of(1)
    rows_of(2)
    pass_on(0)
    arrive(2, 3)
    chunk(quads[0], True)
    pass_on(1)
    go(whole(12, 4, 8))
    go(whole(13, 5, 9))
    arrive(6, 7)
    go(whole(14, 6, 10))
    go(whole(15, 7, 11))
    chunk(quads[1])
    for half in range(2):
        for u in (12, 13):
            ring(0, u, u, half, sibling).wait_recv()
            go(ring(4 + 2 * half + u, u, u + 2, half, sibling))
        if half == 0:
            arrive(8, 9, 10, 11)
            chunk(quads[2])
    for half in range(2):
        for u in (14, 15):
            ring(0, u, u, half, sibling).wait_recv()
        if half == 0:
            chunk(ends[0])
    pick(ends[1])
    early = list(sends)
    sends.clear()
    for p in (0, 2, 1):
        send_picks(p)
    chunk(ends[1], False, False)
    for p in (0, 2, 1):
        send_part(p)
    for copy in early:
        copy.wait_send()
    squashed = jnp.tanh(feats[...].astype(F32) / scale)
    student = (scale * squashed).astype(BF16).astype(F32)
    slope = 1.0 - squashed * squashed
    for p in (0, 2, 1):
        merge_picks(p)
    for p in (0, 2, 1):
        merge_part(p)
    both = last_shares(2)
    done = [finish_part(0, *both), finish_part(1, *last_shares(1)), finish_part(2, *both)]
    mean, hit, lse = [jnp.concatenate([done[0][n], done[2][n], done[1][n]], axis=0) for n in range(3)]
    grad_out[...] = (mean - hit) * slope
    column = lse - jnp.sum(student * hit, axis=1, keepdims=True)
    loss_out[...] = jnp.sum(jnp.where(eye, column, 0.0), axis=0, keepdims=True)

    for copy in sends:
        copy.wait_send()


def body(features, scale_exponents, targets, centres):
    def dma(*shape):
        return pltpu.SemaphoreType.DMA(shape)

    def per_part(make):
        return [make(FIRST[p], SECOND[p]) for p in range(3)]

    loss, grad = pl.pallas_call(
        kernel,
        out_shape=(jax.ShapeDtypeStruct((1, 128), F32), jax.ShapeDtypeStruct((OWN, D), F32)),
        in_specs=[pl.BlockSpec(memory_space=pl.ANY)] * 4,
        out_specs=(pl.BlockSpec(memory_space=pltpu.VMEM), pl.BlockSpec(memory_space=pltpu.VMEM)),
        scratch_shapes=[
            pltpu.SMEM((D // QB,), jnp.int32),
            pltpu.SMEM((OWN,), jnp.int32),
            pltpu.VMEM((OWN, D), BF16),
            pltpu.VMEM((UNITS, HALF, D), BF16),
            pltpu.VMEM((NL, 1, 128), jnp.int32),
            pltpu.VMEM((ROWS, D), BF16),
            pltpu.VMEM((ROWS, 128), jnp.int32),
            pltpu.VMEM((ROWS, 128), F32),
            pltpu.VMEM((ROWS, 128), F32),
            pltpu.VMEM((ROWS, D), F32),
            pltpu.VMEM((ROWS, D), F32),
            *per_part(lambda a, b: pltpu.VMEM((NL, 16, 128), BF16)),
            *per_part(lambda a, b: pltpu.VMEM((NL, 16, 128), BF16)),
            *per_part(lambda a, b: pltpu.VMEM((NL, 16, 128), BF16)),
            *per_part(lambda a, b: pltpu.VMEM((b, 8, 128), F32)),
            *per_part(lambda a, b: pltpu.VMEM((b - 1, a, 16, 128), BF16)),
            *per_part(lambda a, b: pltpu.VMEM((b - 1, a, 16, 128), BF16)),
            *per_part(lambda a, b: pltpu.VMEM((b - 1, 8, 128), F32)),
            *per_part(lambda a, b: pltpu.VMEM((a, 16, 128), BF16)),
            *per_part(lambda a, b: pltpu.VMEM((a, 16, 128), BF16)),
            *per_part(lambda a, b: pltpu.VMEM((8, 128), F32)),
            *per_part(lambda a, b: pltpu.VMEM((a - 1, 16, 128), BF16)),
            *per_part(lambda a, b: pltpu.VMEM((a - 1, 16, 128), BF16)),
            *per_part(lambda a, b: pltpu.VMEM((a - 1, 8, 128), F32)),
            *per_part(lambda a, b: dma(3 * (a + b - 2))),
            *per_part(lambda a, b: dma(3 * (a + b - 2))),
            *per_part(lambda a, b: dma(b - 1)),
            *per_part(lambda a, b: dma(b - 1)),
            *per_part(lambda a, b: dma(a - 1)),
            *per_part(lambda a, b: dma(a - 1)),
            dma(3),
            dma(2),
            dma(20),
            dma(2 * UNITS),
            dma(NX + NZ - 2),
            dma(NX + NZ - 2),
        ],
        compiler_params=pltpu.CompilerParams(
            collective_id=0, has_side_effects=True, vmem_limit_bytes=60 * 1024 * 1024
        ),
    )(scale_exponents, targets, features, centres)
    return loss[0, :OWN], grad


def solution(mesh):
    placed = (P(("loop", "group"), None), P(), P(("loop", "group")), P(("loop", "group"), None))
    return jax.shard_map(
        body,
        mesh=mesh,
        in_specs=placed,
        out_specs=(P(("loop", "group")), P(("loop", "group"), None)),
        check_vma=False,
    )
```
